32 devices in a mesh: row: 4 (over y, core), col: 4 (over z), wave: 2 (over x).
Axes of the slice: x: 2, y: 2, z: 4, core: 2. Of those that a mesh axis runs over, the one named last changes fastest.
Arguments:
- lower_panel: float32 [16, 64, 512], P('wave', None, 'col'), may hold values from -1.5 to 1.5
- diag_inverse: float32 [16, 64, 64], P('wave'), may hold values from -0.75 to 0.75
- ancestor_inverse: float32 [2048, 2048], P('row', ('col', 'wave')), may hold values from -0.375 to 0.375
- pattern: int32 [16, 4], P('wave'), may hold values from 0 to 15, as said below
Outputs:
- inverse_panel: float32 [16, 64, 2048], P('wave', None, ('row', 'col'))
- diag_block: float32 [16, 64, 64], P('wave')
The draws below stay inside these ranges and needn't reach their ends.
Inputs may be any that keep to these rules, and one draw needn't show every extreme that they name: `pattern`: each row holds 4 different block numbers in rising order, and every row includes 0, 15 and half of 16.
All inputs are finite; a program needn't handle non-finite values.
Results may differ from the reference program's by a relative error of at most 0.000096.
Values sent between devices are 32-bit elements; how exact they have to be, the bound alone decides.
No kernel may reach another device: no remote copies, remote signals or barrier semaphores. Data moves between devices by JAX's collectives and lax.ppermute only.
A program may use at most 128 MiB of HBM per device.

```python
import jax
import jax.numpy as jnp
from jax import lax

W = 64
BLK = 128
SIBS = 16
ANCESTOR_BLOCKS = 16
NBK = 4
R = 2048


def shuffled(key_one):
    return jax.random.permutation(key_one, ANCESTOR_BLOCKS).astype(jnp.int32)


def draw_pattern(key, part):
    key_perm = jax.random.fold_in(key, 11)
    group_key = jax.random.fold_in(key, 12)
    extra_score_group = jax.random.randint(group_key, (ANCESTOR_BLOCKS // 8,), 0, 4).astype(jnp.int32)
    extra_score_full = jnp.repeat(extra_score_group, 8)
    key_list = jax.random.split(key_perm, SIBS)
    block_orders = jax.vmap(shuffled)(key_list)
    blocks = jnp.arange(ANCESTOR_BLOCKS, dtype=jnp.int32)
    needed = (blocks == 0) | (blocks == ANCESTOR_BLOCKS - 1) | (blocks == ANCESTOR_BLOCKS // 2)
    required_choice = jnp.where(needed, 8, 0).astype(jnp.int32)
    block_scores = (extra_score_full + required_choice)[None, :] * ANCESTOR_BLOCKS + block_orders
    values_top, chosen = lax.top_k(block_scores, NBK)
    return jnp.sort(chosen, axis=1).astype(jnp.int32)


def raised(drawn, stream_key, source, target, parts, factor):
    owner, partner = [(jnp.arange(drawn.shape[dim]) // (drawn.shape[dim] // parts)).reshape([-1 if axis == dim else 1 for axis in range(drawn.ndim)]) for dim in (source, target)]
    chosen = jax.random.permutation(stream_key, parts)[partner]
    strong = (owner == chosen) | (owner == (partner + parts // 2) % parts)
    return jnp.where(strong, factor * drawn, drawn)


def shard_levels(own_key, dims, cuts, least, high):
    loudness = 1.0
    for dim, blocks in cuts:
        draws = jax.random.uniform(jax.random.fold_in(jax.random.fold_in(own_key, 6), dim), (blocks,), jnp.float32, least / len(cuts), high / len(cuts))
        loudness = loudness * jnp.repeat(jnp.exp(draws), dims[dim] // blocks).reshape((-1,) + (1,) * (len(dims) - 1 - dim))
    return loudness


def gaussian(rng, shape, width, limit, cuts=(), kind=jnp.bfloat16):
    loudness = shard_levels(rng, shape, cuts, -0.22, 0.18) if cuts else 1.0
    entries = jax.random.normal(rng, shape, jnp.float32) * width * loudness
    return jnp.minimum(jnp.maximum(entries, -limit), limit).astype(kind)


def bell_draw_with(own_key, shape, width, most, cuts, heavy, held_as=jnp.bfloat16):
    result = width * jax.random.normal(own_key, shape, jnp.float32)
    if cuts:
        result = result * shard_levels(own_key, shape, cuts, -0.22, 0.18)
    return jnp.clip(raised(result, jax.random.fold_in(own_key, 3), *heavy), -most, most).astype(held_as)


def setup_inputs(seed: int = 0) -> dict:
    arg_keys = jax.random.split(jax.random.key(seed), 5)
    lower_panel = gaussian(arg_keys[0], (SIBS, W, NBK * BLK), 0.25, 1.5, ((0, 2), (2, 4)), jnp.float32)
    diag_inverse = gaussian(arg_keys[1], (SIBS, W, W), W ** -0.5, 0.75, ((0, 2),), jnp.float32)
    ancestor_inverse = bell_draw_with(arg_keys[2], (R, R), (NBK * BLK) ** -0.5, 0.375, ((0, 4), (1, 8)), (1, 0, 8, 2.0), jnp.float32)
    pattern = draw_pattern(jax.random.fold_in(arg_keys[4], 71), 0)
    return {"lower_panel": lower_panel, "diag_inverse": diag_inverse, "ancestor_inverse": ancestor_inverse, "pattern": pattern}


def reference(lower_panel, diag_inverse, ancestor_inverse, pattern):
    highest = lax.Precision.HIGHEST
    normed = jnp.einsum("svw,svk->swk", diag_inverse, lower_panel, precision=highest)
    packed = normed.reshape(SIBS, W, NBK, BLK)
    blocks = jnp.arange(ANCESTOR_BLOCKS, dtype=jnp.int32)
    onehot = (pattern[:, None, :] == blocks[None, :, None]).astype(jnp.float32)
    dense_panel = jnp.einsum("sqk,swkb->swqb", onehot, packed, precision=highest).reshape(SIBS * W, ANCESTOR_BLOCKS * BLK)
    product = lax.dot_general(dense_panel, ancestor_inverse, (((1,), (1,)), ((), ())), precision=highest)
    row_mask = jnp.repeat(jnp.sum(onehot, axis=2), BLK, axis=1)
    inverse_panel = -product.reshape(SIBS, W, ANCESTOR_BLOCKS * BLK) * row_mask[:, None, :]
    base_block = jnp.einsum("svw,svx->swx", diag_inverse, diag_inverse, precision=highest)
    update = jnp.einsum("swr,sxr->swx", dense_panel.reshape(SIBS, W, ANCESTOR_BLOCKS * BLK), inverse_panel, precision=highest)
    return inverse_panel, base_block - update
```

```python
import functools

import jax
import jax.numpy as jnp
from jax import lax
from jax.experimental import pallas as pl
from jax.experimental.pallas import tpu as pltpu
from jax.sharding import PartitionSpec as P

BLK = 128


def xor_permute(value, axis, distance):
    return lax.ppermute(value, axis, [(i, i ^ distance) for i in range(lax.axis_size(axis))])


def split(value):
    high = value.astype(jnp.bfloat16)
    return high, (value - high.astype(jnp.float32)).astype(jnp.bfloat16)


def product(left, right, dims):
    dot = functools.partial(lax.dot_general, dimension_numbers=(dims, ((), ())), preferred_element_type=jnp.float32)
    return dot(left[0], right[0]) + (dot(left[0], right[1]) + dot(left[1], right[0]))


def local_kernel(n_col, sibs, slots, nbk, col_blocks, pattern, ids, dinv, *refs):
    own_panel = refs[0]
    halves = refs[1:n_col]
    core_halves = refs[n_col : 2 * n_col - 1]
    mine = refs[2 * n_col - 1 : 3 * n_col - 1]
    theirs = refs[3 * n_col - 1 : 4 * n_col - 1]
    panel_out, keep_out, send_out, l_high, l_low, a_high, a_low, update = refs[4 * n_col - 1 :]
    col_id, wave_id, core, block, base_here = ids[0], ids[1], ids[2], ids[3], ids[4]
    half = sibs // 2

    def put_panel(ref, first, count, owner):
        for slot in range(slots):
            high, low = split(ref[:, :, slot * BLK : (slot + 1) * BLK])
            l_high[owner * slots + slot, pl.ds(first, count)] = high
            l_low[owner * slots + slot, pl.ds(first, count)] = low

    put_panel(own_panel, 0, sibs, col_id)
    for step in range(1, n_col):
        put_panel(halves[step - 1], core * half, half, col_id ^ step)
        put_panel(core_halves[step - 1], (1 - core) * half, half, col_id ^ step)
    for step in range(n_col):
        for group, pieces in ((wave_id, mine), (1 - wave_id, theirs)):
            for part in range(col_blocks):
                high, low = split(pieces[step][:, part * BLK : (part + 1) * BLK])
                place = ((col_id ^ step) * 2 + group) * col_blocks + part
                a_high[place] = high
                a_low[place] = low

    def sibling(s, carry):
        total = jnp.zeros((dinv.shape[1], BLK), jnp.float32)
        found, slot = False, 0
        width = min(4, nbk)
        for first in range(0, nbk, width):
            places = [pattern[s, first + k] for k in range(width)]
            left = tuple(jnp.concatenate([ref[first + k, s] for k in range(width)], axis=1) for ref in (l_high, l_low))
            right = tuple(jnp.concatenate([ref[place] for place in places], axis=1) for ref in (a_high, a_low))
            total = total + product(left, right, ((1,), (1,)))
            for k, place in enumerate(places):
                hit = place == block
                slot = jnp.where(hit, first + k, slot)
                found = jnp.logical_or(found, hit)
        inverse = dinv[s]
        factor = split(inverse)
        kept = jnp.where(found, -1.0, 0.0)
        panel = product(factor, split(total), ((0,), (0,))) * kept
        panel_out[s] = panel
        normed = product(factor, (l_high[slot, s], l_low[slot, s]), ((0,), (0,)))
        step = product(split(normed), split(panel), ((1,), (1,)))
        base = product(factor, factor, ((0,), (0,)))
        update[s] = base * jnp.where(base_here == 1, 1.0, 0.0) - step
        return carry

    if sibs * nbk <= 64:
        for s in range(sibs):
            sibling(s, 0)
    else:
        lax.fori_loop(0, sibs, sibling, 0)
    quarter = sibs // 4
    for out, part in ((keep_out, core), (send_out, 1 - core)):
        for i in range(quarter):
            pair = part * half + i
            out[i] = jnp.concatenate([update[pair], update[pair + quarter]], axis=1)


def per_device(lower_panel, diag_inverse, ancestor_inverse, pattern):
    sibs, width, packed = lower_panel.shape
    rows_here, cols_here = ancestor_inverse.shape
    n_row, n_col = lax.axis_size("row"), lax.axis_size("col")
    row_id, col_id, wave_id = (lax.axis_index(axis) for axis in ("row", "col", "wave"))
    core = row_id % 2
    own_rows = rows_here // n_col
    slots, col_blocks, nbk = packed // BLK, cols_here // BLK, pattern.shape[1]
    half, quarter = sibs // 2, sibs // 4

    panel_half = lax.dynamic_slice_in_dim(lower_panel, core * half, half, 0)
    halves = {0: panel_half}
    bit = n_col // 2
    while bit:
        for step in list(halves):
            halves[step ^ bit] = xor_permute(halves[step], "col", bit)
        bit //= 2
    core_halves = {step: xor_permute(halves[step], "row", 1) for step in range(1, n_col)}

    chunks = [
        lax.dynamic_slice_in_dim(ancestor_inverse, (col_id ^ step) * own_rows, own_rows, 0) for step in range(n_col)
    ]
    mine = [chunks[0]] + [xor_permute(chunks[step], "col", step) for step in range(1, n_col)]
    theirs = [xor_permute(piece, "wave", 1) for piece in mine]

    ids = jnp.stack(
        [col_id, wave_id, core, row_id * n_col + col_id, jnp.where((row_id == 0) & (col_id == 0), 1, 0)]
    ).astype(jnp.int32)
    operands = [lower_panel]
    operands += [halves[step] for step in range(1, n_col)] + [core_halves[step] for step in range(1, n_col)]
    operands += mine + theirs
    smem = pl.BlockSpec(memory_space=pltpu.SMEM)
    vmem = pl.BlockSpec(memory_space=pltpu.VMEM)
    n_blocks = n_col * 2 * col_blocks
    panel, keep, send = pl.pallas_call(
        functools.partial(local_kernel, n_col, sibs, slots, nbk, col_blocks),
        out_shape=(
            jax.ShapeDtypeStruct((sibs, width, BLK), jnp.float32),
            jax.ShapeDtypeStruct((quarter, width, 2 * width), jnp.float32),
            jax.ShapeDtypeStruct((quarter, width, 2 * width), jnp.float32),
        ),
        in_specs=[smem, smem] + [vmem] * (1 + len(operands)),
        out_specs=(vmem, vmem, vmem),
        scratch_shapes=[
            pltpu.VMEM((n_col * slots, sibs, width, BLK), jnp.bfloat16),
            pltpu.VMEM((n_col * slots, sibs, width, BLK), jnp.bfloat16),
            pltpu.VMEM((n_blocks, BLK, BLK), jnp.bfloat16),
            pltpu.VMEM((n_blocks, BLK, BLK), jnp.bfloat16),
            pltpu.VMEM((sibs, width, width), jnp.float32),
        ],
        compiler_params=pltpu.CompilerParams(vmem_limit_bytes=48 * 2**20),
    )(pattern, ids, diag_inverse, *operands)

    total = keep + xor_permute(send, "row", 1)
    bit = 2
    while bit < n_row:
        total = total + xor_permute(total, "row", bit)
        bit *= 2
    bit = 1
    while bit < n_col:
        total = total + xor_permute(total, "col", bit)
        bit *= 2
    other = xor_permute(total, "row", 1)
    first = jnp.where(core == 0, total, other)
    second = jnp.where(core == 0, other, total)
    both = jnp.concatenate([first[..., :width], first[..., width:], second[..., :width], second[..., width:]], axis=0)
    return panel, both


def solution(mesh):
    return jax.shard_map(
        per_device,
        mesh=mesh,
        in_specs=(
            P("wave", None, "col"),
            P("wave", None, None),
            P("row", ("col", "wave")),
            P("wave", None),
        ),
        out_specs=(P("wave", None, ("row", "col")), P("wave", None, None)),
        check_vma=False,
    )
```

```python
import functools

import jax
import jax.numpy as jnp
from jax import lax
from jax.experimental import pallas as pl
from jax.experimental.pallas import tpu as pltpu
from jax.sharding import PartitionSpec as P

BLK = 128
CONTRACT_LAST = ((1,), (1,))
CONTRACT_FIRST = ((0,), (0,))


DONE = {'core_own': 1, 'mine0': 5, 'mine1': 4, 'mine2': 4, 'normed_other': 4, 'panel': 6, 'theirs0': 4, 'theirs1': None, 'theirs2': None}
GATE = {'mine2': False, 'scalars': True}
SPLIT = True
COST = [100000000000, 1000000000, 100000000000]


def xor_permute(value, axis, distance):
    return lax.ppermute(value, axis, [(i, i ^ distance) for i in range(lax.axis_size(axis))])


def split(value):
    high = value.astype(jnp.bfloat16)
    return high, (value - high.astype(jnp.float32)).astype(jnp.bfloat16)


def product(left, right, dims):
    dot = functools.partial(lax.dot_general, dimension_numbers=(dims, ((), ())), preferred_element_type=jnp.float32)
    return dot(left[0], right[0]) + (dot(left[0], right[1]) + dot(left[1], right[0]))


def update_kernel(n_col, slots, col_blocks, rows_blocks, scalars, dinv, *refs):
    halves, (own, partner, core_own, core_partner) = refs[:n_col], refs[n_col : n_col + 4]
    out, normed_out, r_high, r_low, c_high, c_low = refs[n_col + 4 :]
    nbk = n_col * slots
    col_id, wave_id, core, row_id = scalars[scalars.shape[0] - 5 + 0], scalars[scalars.shape[0] - 5 + 1], scalars[scalars.shape[0] - 5 + 2], scalars[scalars.shape[0] - 5 + 3]
    half, width = halves[0].shape[0], halves[0].shape[1]
    row_first = (row_id - core) * rows_blocks
    col_first = col_id * 2 * col_blocks
    n_rows, n_cols = 2 * rows_blocks, 2 * col_blocks
    for ref in (r_high, r_low, c_high, c_low):
        ref[...] = jnp.zeros_like(ref)
    for s in range(half):
        lower = jnp.concatenate([halves[step][s] for step in range(n_col)], axis=1)
        normed = product(split(dinv[core * half + s]), split(lower), CONTRACT_FIRST)
        for step in range(n_col):
            for slot in range(slots):
                first = (step * slots + slot) * BLK
                here = normed[:, first : first + BLK]
                number = (col_id ^ step) * slots + slot
                normed_out[number, s] = here
                high, low = split(here)
                place = scalars[(core * half + s) * nbk + number]
                for first, count, to_high, to_low in ((row_first, n_rows, r_high, r_low), (col_first, n_cols, c_high, c_low)):
                    inside = jnp.logical_and(place >= first, place < first + count)
                    target = jnp.where(inside, place - first, count)
                    to_high[target, s * width : (s + 1) * width] = high
                    to_low[target, s * width : (s + 1) * width] = low

    def columns(ref):
        mine = [ref[wave_id * col_blocks + part] for part in range(col_blocks)]
        theirs = [ref[(1 - wave_id) * col_blocks + part] for part in range(col_blocks)]
        return jnp.concatenate(mine + theirs, axis=1)

    left = columns(c_high), columns(c_low)
    total = jnp.zeros((half * width, half * width), jnp.float32)
    group = 2
    for who, mine, theirs in ((core, own, partner), (1 - core, core_own, core_partner)):
        for first in range(0, rows_blocks, group):
            rows = slice(first * BLK, (first + group) * BLK)
            block = split(jnp.concatenate([mine[rows, :], theirs[rows, :]], axis=1))
            part = product(left, block, CONTRACT_LAST)
            place = who * rows_blocks + first
            right = tuple(jnp.concatenate([ref[place + i] for i in range(group)], axis=1) for ref in (r_high, r_low))
            total = total + product(right, split(part), CONTRACT_LAST)
    blocks = [total[s * width : (s + 1) * width, s * width : (s + 1) * width] for s in range(half)]
    for i in range(half // 2):
        out[i] = jnp.concatenate([blocks[i], blocks[i + half // 2]], axis=1)


def add_products(total, left, r_high, r_low, blocks):
    for place, rows in blocks:
        part = product(left, split(rows), CONTRACT_LAST)
        right = tuple(jnp.concatenate([ref[place], ref[place + 1]], axis=1) for ref in (r_high, r_low))
        total = total + product(right, split(part), CONTRACT_LAST)
    return total


def row_pairs(core, rows_blocks, own, other):
    for who, ref in ((core, own), (1 - core, other)):
        for first in range(0, rows_blocks, 2):
            yield who * rows_blocks + first, ref[first * BLK : (first + 2) * BLK, :]


def columns(ref, first, count):
    return jnp.concatenate([ref[first + part] for part in range(count)], axis=1)


def first_kernel(n_col, slots, col_blocks, rows_blocks, scalars, dinv, *refs):
    halves, own, core_own = refs[:n_col], refs[n_col], refs[n_col + 1]
    total_out, normed_out, r_high, r_low, c_high, c_low = refs[n_col + 2 :]
    nbk = n_col * slots
    col_id, wave_id, core, row_id = scalars[scalars.shape[0] - 5 + 0], scalars[scalars.shape[0] - 5 + 1], scalars[scalars.shape[0] - 5 + 2], scalars[scalars.shape[0] - 5 + 3]
    half, width = halves[0].shape[0], halves[0].shape[1]
    row_first = (row_id - core) * rows_blocks
    col_first = col_id * 2 * col_blocks
    n_rows, n_cols = 2 * rows_blocks, 2 * col_blocks
    for ref in (r_high, r_low, c_high, c_low):
        ref[...] = jnp.zeros_like(ref)
    for s in range(half):
        lower = jnp.concatenate([halves[step][s] for step in range(n_col)], axis=1)
        normed = product(split(dinv[core * half + s]), split(lower), CONTRACT_FIRST)
        for step in range(n_col):
            for slot in range(slots):
                first = (step * slots + slot) * BLK
                here = normed[:, first : first + BLK]
                number = (col_id ^ step) * slots + slot
                normed_out[number, s] = here
                high, low = split(here)
                place = scalars[(core * half + s) * nbk + number]
                for first, count, to_high, to_low in ((row_first, n_rows, r_high, r_low), (col_first, n_cols, c_high, c_low)):
                    inside = jnp.logical_and(place >= first, place < first + count)
                    target = jnp.where(inside, place - first, count)
                    to_high[target, s * width : (s + 1) * width] = high
                    to_low[target, s * width : (s + 1) * width] = low
    left = tuple(columns(ref, wave_id * col_blocks, col_blocks) for ref in (c_high, c_low))
    total = jnp.zeros((half * width, half * width), jnp.float32)
    total_out[...] = add_products(total, left, r_high, r_low, row_pairs(core, rows_blocks, own, core_own))


def second_kernel(half, width, col_blocks, rows_blocks, scalars, total, r_high, r_low, c_high, c_low, partner, core_partner, out):
    wave_id, core = scalars[scalars.shape[0] - 5 + 1], scalars[scalars.shape[0] - 5 + 2]
    left = tuple(columns(ref, (1 - wave_id) * col_blocks, col_blocks) for ref in (c_high, c_low))
    total = add_products(total[...], left, r_high, r_low, row_pairs(core, rows_blocks, partner, core_partner))
    blocks = [total[s * width : (s + 1) * width, s * width : (s + 1) * width] for s in range(half)]
    for i in range(half // 2):
        out[i] = jnp.concatenate([blocks[i], blocks[i + half // 2]], axis=1)


def panel_kernel(n_col, sibs, nbk, col_blocks, scalars, dinv, *refs):
    normed, own, partner = refs[:2], refs[2], refs[3]
    mine, theirs = refs[4 : 3 + n_col], refs[3 + n_col : 2 + 2 * n_col]
    panel_out, base_out, n_high, n_low, a_high, a_low = refs[2 + 2 * n_col :]
    col_id, wave_id, core, block = scalars[scalars.shape[0] - 5 + 0], scalars[scalars.shape[0] - 5 + 1], scalars[scalars.shape[0] - 5 + 2], scalars[scalars.shape[0] - 5 + 4]
    half = sibs // 2
    for ref, who in zip(normed, (core, 1 - core)):
        for slot in range(nbk):
            high, low = split(ref[slot])
            n_high[slot, pl.ds(who * half, half)] = high
            n_low[slot, pl.ds(who * half, half)] = low
    here = pl.ds(pl.multiple_of(col_id * BLK, BLK), BLK)
    for step in range(n_col):
        for group, first, pieces in ((wave_id, own, mine), (1 - wave_id, partner, theirs)):
            for part in range(col_blocks):
                columns = slice(part * BLK, (part + 1) * BLK)
                high, low = split(pieces[step - 1][:, columns] if step else first[here, columns])
                place = ((col_id ^ step) * 2 + group) * col_blocks + part
                a_high[place] = high
                a_low[place] = low

    def sibling(s, carry):
        total = jnp.zeros((dinv.shape[1], BLK), jnp.float32)
        found = False
        width = min(4, nbk)
        for first in range(0, nbk, width):
            places = [scalars[(s) * nbk + first + k] for k in range(width)]
            left = tuple(jnp.concatenate([ref[first + k, s] for k in range(width)], axis=1) for ref in (n_high, n_low))
            right = tuple(jnp.concatenate([ref[place] for place in places], axis=1) for ref in (a_high, a_low))
            total = total + product(left, right, CONTRACT_LAST)
            for place in places:
                found = jnp.logical_or(found, place == block)
        panel_out[s] = total * jnp.where(found, -1.0, 0.0)
        return carry

    if sibs * nbk <= 64:
        for s in range(sibs):
            sibling(s, 0)
    else:
        lax.fori_loop(0, sibs, sibling, 0)
    bases = []
    for s in range(sibs):
        factor = split(dinv[s])
        bases.append(product(factor, factor, CONTRACT_FIRST))
    for i in range(half // 2):
        for first in (0, half):
            base_out[first // 2 + i] = jnp.concatenate([bases[first + i], bases[first + half // 2 + i]], axis=1)


def per_device(lower_panel, diag_inverse, ancestor_inverse, pattern):
    sibs, width, packed = lower_panel.shape
    rows_here, cols_here = ancestor_inverse.shape
    n_row, n_col = lax.axis_size("row"), lax.axis_size("col")
    row_id, col_id, wave_id = (lax.axis_index(axis) for axis in ("row", "col", "wave"))
    core = row_id % 2
    own_rows = rows_here // n_col
    slots, col_blocks, nbk = packed // BLK, cols_here // BLK, pattern.shape[1]
    rows_blocks = rows_here // BLK
    half, quarter = sibs // 2, sibs // 4
    n_blocks = n_col * 2 * col_blocks
    f32, bf16 = jnp.float32, jnp.bfloat16
    smem = pl.BlockSpec(memory_space=pltpu.SMEM)
    vmem = pl.BlockSpec(memory_space=pltpu.VMEM)
    mib = 2**20
    size = rows_here * cols_here * 4 // mib + 1
    params = pltpu.CompilerParams(vmem_limit_bytes=min(60, 12 + 12 * size) * mib)
    ids = jnp.stack([col_id, wave_id, core, row_id, row_id * n_col + col_id]).astype(jnp.int32)

    def call(kernel, out_shape, operands, scratch, flops):
        moved = sum(x.size * 4 for x in operands)
        return pl.pallas_call(
            kernel,
            out_shape=out_shape,
            in_specs=[smem] + [vmem] * len(operands),
            out_specs=jax.tree.map(lambda _: vmem, out_shape),
            scratch_shapes=scratch,
            compiler_params=params,
            cost_estimate=pl.CostEstimate(flops=flops, bytes_accessed=(moved if flops > 10 else 1), transcendentals=0),
        )(scalars, *operands)

    def tie(point, value):
        names = [name for name in late if due(name) == point]
        if names:
            value, *tied = lax.optimization_barrier((value, *[late[name] for name in names]))
            late.update(zip(names, tied))
        return value

    def due(name):
        if name[-1].isdigit():
            stem = name.rstrip("0123456789")
            return DONE.get(stem + str(min(int(name[len(stem) :]), 2)))
        return DONE.get(name)

    far = n_col // 2
    late = {}
    half_panel = lax.dynamic_slice_in_dim(lower_panel, core * half, half, 0)
    source = ancestor_inverse
    if GATE.get("wave"):
        source, half_panel = lax.optimization_barrier((source, half_panel))
    partner = xor_permute(source, "wave", 1)
    halves = {0: half_panel}
    halves[far] = xor_permute(halves[0], "col", far)
    chunks = [
        lax.dynamic_slice_in_dim(ancestor_inverse, (col_id ^ step) * own_rows, own_rows, 0) for step in range(1, n_col)
    ]
    if GATE.get("slices"):
        half_panel, *chunks = lax.optimization_barrier((half_panel, *chunks))
        halves[0] = half_panel
        halves[far] = xor_permute(half_panel, "col", far)
    gated = [i for i in range(n_col - 1) if GATE.get("mine" + str(min(i, 2)))]
    if gated:
        halves[far], *held = lax.optimization_barrier((halves[far], *[chunks[i] for i in gated]))
        for i, chunk in zip(gated, held):
            chunks[i] = chunk
    mine = [xor_permute(chunk, "col", step) for step, chunk in enumerate(chunks, 1)]
    late.update({"mine" + str(i): x for i, x in enumerate(mine)})
    late.update({"theirs" + str(i): xor_permute(x, "wave", 1) for i, x in enumerate(mine)})
    late["core_own"] = xor_permute(ancestor_inverse, "row", 1)
    scalars = jnp.concatenate([pattern.reshape(-1), ids])
    if GATE.get("scalars"):
        halves[far], scalars = lax.optimization_barrier((halves[far], scalars))
    halves[far] = tie(0, halves[far])
    bit = far // 2
    while bit:
        for step in list(halves):
            halves[step ^ bit] = xor_permute(halves[step], "col", bit)
        bit //= 2
    partner, *tied = lax.optimization_barrier((partner, *[halves[step] for step in range(n_col)]))
    halves = dict(enumerate(tied))
    partner = tie(1, partner)
    core_partner = xor_permute(partner, "row", 1)
    if SPLIT:
        square = half * width
        partial, normed, *placed = call(
            functools.partial(first_kernel, n_col, slots, col_blocks, rows_blocks),
            (
                jax.ShapeDtypeStruct((square, square), f32),
                jax.ShapeDtypeStruct((nbk, half, width, BLK), f32),
                jax.ShapeDtypeStruct((2 * rows_blocks + 1, square, BLK), bf16),
                jax.ShapeDtypeStruct((2 * rows_blocks + 1, square, BLK), bf16),
                jax.ShapeDtypeStruct((2 * col_blocks + 1, square, BLK), bf16),
                jax.ShapeDtypeStruct((2 * col_blocks + 1, square, BLK), bf16),
            ),
            [diag_inverse] + [halves[step] for step in range(n_col)] + [ancestor_inverse, late["core_own"]],
            [],
            COST[0],
        )
        late["normed_other"] = xor_permute(normed, "row", 1)
        core_partner = tie(2, core_partner)
        total = call(
            functools.partial(second_kernel, half, width, col_blocks, rows_blocks),
            jax.ShapeDtypeStruct((quarter, width, 2 * width), f32),
            [partial, *placed, partner, core_partner],
            [],
            COST[2],
        )
    else:
        core_partner = tie(2, core_partner)
        total, normed = call(
            functools.partial(update_kernel, n_col, slots, col_blocks, rows_blocks),
            (
                jax.ShapeDtypeStruct((quarter, width, 2 * width), f32),
                jax.ShapeDtypeStruct((nbk, half, width, BLK), f32),
            ),
            [diag_inverse] + [halves[step] for step in range(n_col)]
            + [ancestor_inverse, partner, late["core_own"], core_partner],
            [pltpu.VMEM((2 * rows_blocks + 1, half * width, BLK), bf16)] * 2
            + [pltpu.VMEM((2 * col_blocks + 1, half * width, BLK), bf16)] * 2,
            COST[0],
        )
        late["normed_other"] = xor_permute(normed, "row", 1)
    total = tie(3, total)
    bit = 2
    while bit < n_row:
        total = total + xor_permute(total, "row", bit)
        bit *= 2
    total = tie(4, total)
    bit = 1
    while bit < n_col:
        total = total + xor_permute(total, "col", bit)
        bit *= 2
        if bit < n_col:
            total = tie(5, total)
    total = tie(6, total)
    pieces = [late["mine" + str(i)] for i in range(n_col - 1)] + [late["theirs" + str(i)] for i in range(n_col - 1)]
    panel, base = call(
        functools.partial(panel_kernel, n_col, sibs, nbk, col_blocks),
        (
            jax.ShapeDtypeStruct((sibs, width, BLK), f32),
            jax.ShapeDtypeStruct((half, width, 2 * width), f32),
        ),
        [diag_inverse, normed, late["normed_other"], ancestor_inverse, partner] + pieces,
        [pltpu.VMEM((nbk, sibs, width, BLK), bf16)] * 2 + [pltpu.VMEM((n_blocks, BLK, BLK), bf16)] * 2,
        COST[1],
    )
    if DONE.get("panel") == 6:
        total, panel = lax.optimization_barrier((total, panel))
    other = xor_permute(total, "row", 1)
    if DONE.get("panel") == 7:
        other, panel = lax.optimization_barrier((other, panel))
    first = jnp.where(core == 0, total, other) + base[:quarter]
    second = jnp.where(core == 0, other, total) + base[quarter:]
    diag = jnp.concatenate([first[..., :width], first[..., width:], second[..., :width], second[..., width:]], axis=0)
    return panel, diag


def solution(mesh):
    return jax.shard_map(
        per_device,
        mesh=mesh,
        in_specs=(
            P("wave", None, "col"),
            P("wave", None, None),
            P("row", ("col", "wave")),
            P("wave", None),
        ),
        out_specs=(P("wave", None, ("row", "col")), P("wave", None, None)),
        check_vma=False,
    )
```

```python
import functools

import jax
import jax.numpy as jnp
from jax import lax
from jax.experimental import pallas as pl
from jax.experimental.pallas import tpu as pltpu
from jax.sharding import PartitionSpec as P

BLK = 128
CONTRACT_LAST = ((1,), (1,))
CONTRACT_FIRST = ((0,), (0,))


DONE = {'core_own': 2, 'mine0': 2, 'mine1': 4, 'mine2': 3, 'normed_other': 4, 'panel': 6, 'prep': 5, 'theirs0': 5, 'theirs1': None, 'theirs2': None}
GATE = {'mine0': 0, 'mine2': False, 'scalars': True}
SPLIT = True
RADIX = False
MIX = False
TIED = False
COST = [100000000000, 100000000000, 100000000000]


def xor_permute(value, axis, distance):
    return lax.ppermute(value, axis, [(i, i ^ distance) for i in range(lax.axis_size(axis))])


def split(value):
    high = value.astype(jnp.bfloat16)
    return high, (value - high.astype(jnp.float32)).astype(jnp.bfloat16)


def product(left, right, dims):
    dot = functools.partial(lax.dot_general, dimension_numbers=(dims, ((), ())), preferred_element_type=jnp.float32)
    return dot(left[0], right[0]) + (dot(left[0], right[1]) + dot(left[1], right[0]))


def norm_kernel(scalars, dinv, lower, out):
    half = out.shape[0]
    core = scalars[scalars.shape[0] - 3]
    for s in range(half):
        out[s] = packed_product(split(dinv[core * half + s]), split(lower[s]), CONTRACT_FIRST)


def packed_product(left, right, dims):
    axis = 1 - dims[0][0]
    rows, columns = left[0].shape[axis], right[0].shape[axis]
    both = lax.dot_general(
        jnp.concatenate(left, axis=axis),
        jnp.concatenate(right, axis=axis),
        (dims, ((), ())),
        preferred_element_type=jnp.float32,
    )
    return both[:rows, :columns] + (both[:rows, columns:] + both[rows:, :columns])


def update_kernel(n_col, slots, col_blocks, rows_blocks, scalars, dinv, *refs):
    halves, (own, partner, core_own, core_partner) = refs[:n_col], refs[n_col : n_col + 4]
    out, normed_out, r_high, r_low, c_high, c_low = refs[n_col + 4 :]
    nbk = n_col * slots
    col_id, wave_id, core, row_id = scalars[scalars.shape[0] - 5 + 0], scalars[scalars.shape[0] - 5 + 1], scalars[scalars.shape[0] - 5 + 2], scalars[scalars.shape[0] - 5 + 3]
    half, width = halves[0].shape[0], halves[0].shape[1]
    row_first = (row_id - core) * rows_blocks
    col_first = col_id * 2 * col_blocks
    n_rows, n_cols = 2 * rows_blocks, 2 * col_blocks
    for ref in (r_high, r_low, c_high, c_low):
        ref[...] = jnp.zeros_like(ref)
    for s in range(half):
        far = n_col // 2
        lower = jnp.concatenate([halves[step][s] for step in range(far)], axis=1)
        normed = packed_product(split(dinv[core * half + s]), split(lower), CONTRACT_FIRST)
        normed = jnp.concatenate([normed] + [halves[step][s] for step in range(far, n_col)], axis=1)
        for step in range(n_col):
            for slot in range(slots):
                first = (step * slots + slot) * BLK
                here = normed[:, first : first + BLK]
                number = (col_id ^ step) * slots + slot
                normed_out[number, s] = here
                high, low = split(here)
                place = scalars[(core * half + s) * nbk + number]
                for first, count, to_high, to_low in ((row_first, n_rows, r_high, r_low), (col_first, n_cols, c_high, c_low)):
                    inside = jnp.logical_and(place >= first, place < first + count)
                    target = jnp.where(inside, place - first, count)
                    to_high[target, s * width : (s + 1) * width] = high
                    to_low[target, s * width : (s + 1) * width] = low

    def columns(ref):
        mine = [ref[wave_id * col_blocks + part] for part in range(col_blocks)]
        theirs = [ref[(1 - wave_id) * col_blocks + part] for part in range(col_blocks)]
        return jnp.concatenate(mine + theirs, axis=1)

    left = columns(c_high), columns(c_low)
    total = jnp.zeros((half * width, half * width), jnp.float32)
    group = 2
    for who, mine, theirs in ((core, own, partner), (1 - core, core_own, core_partner)):
        for first in range(0, rows_blocks, group):
            rows = slice(first * BLK, (first + group) * BLK)
            block = split(jnp.concatenate([mine[rows, :], theirs[rows, :]], axis=1))
            part = product(left, block, CONTRACT_LAST)
            place = who * rows_blocks + first
            right = tuple(jnp.concatenate([ref[place + i] for i in range(group)], axis=1) for ref in (r_high, r_low))
            total = total + product(right, split(part), CONTRACT_LAST)
    blocks = [total[s * width : (s + 1) * width, s * width : (s + 1) * width] for s in range(half)]
    for i in range(half // 2):
        out[i] = jnp.concatenate([blocks[i], blocks[i + half // 2]], axis=1)


def add_products(total, left, r_high, r_low, blocks):
    for place, rows in blocks:
        part = product(left, split(rows), CONTRACT_LAST)
        right = tuple(jnp.concatenate([ref[place], ref[place + 1]], axis=1) for ref in (r_high, r_low))
        total = total + product(right, split(part), CONTRACT_LAST)
    return total


def row_pairs(core, rows_blocks, own, other):
    for who, ref in ((core, own), (1 - core, other)):
        for first in range(0, rows_blocks, 2):
            yield who * rows_blocks + first, ref[first * BLK : (first + 2) * BLK, :]


def columns(ref, first, count):
    return jnp.concatenate([ref[first + part] for part in range(count)], axis=1)


def first_kernel(n_col, slots, col_blocks, rows_blocks, scalars, dinv, *refs):
    halves, own, core_own = refs[:n_col], refs[n_col], refs[n_col + 1]
    total_out, normed_out, r_high, r_low, c_high, c_low = refs[n_col + 2 :]
    nbk = n_col * slots
    col_id, wave_id, core, row_id = scalars[scalars.shape[0] - 5 + 0], scalars[scalars.shape[0] - 5 + 1], scalars[scalars.shape[0] - 5 + 2], scalars[scalars.shape[0] - 5 + 3]
    half, width = halves[0].shape[0], halves[0].shape[1]
    row_first = (row_id - core) * rows_blocks
    col_first = col_id * 2 * col_blocks
    n_rows, n_cols = 2 * rows_blocks, 2 * col_blocks
    for ref in (r_high, r_low, c_high, c_low):
        ref[...] = jnp.zeros_like(ref)
    for s in range(half):
        far = n_col // 2
        lower = jnp.concatenate([halves[step][s] for step in range(far)], axis=1)
        normed = packed_product(split(dinv[core * half + s]), split(lower), CONTRACT_FIRST)
        normed = jnp.concatenate([normed] + [halves[step][s] for step in range(far, n_col)], axis=1)
        for step in range(n_col):
            for slot in range(slots):
                first = (step * slots + slot) * BLK
                here = normed[:, first : first + BLK]
                number = (col_id ^ step) * slots + slot
                normed_out[number, s] = here
                high, low = split(here)
                place = scalars[(core * half + s) * nbk + number]
                for first, count, to_high, to_low in ((row_first, n_rows, r_high, r_low), (col_first, n_cols, c_high, c_low)):
                    inside = jnp.logical_and(place >= first, place < first + count)
                    target = jnp.where(inside, place - first, count)
                    to_high[target, s * width : (s + 1) * width] = high
                    to_low[target, s * width : (s + 1) * width] = low
    left = tuple(columns(ref, wave_id * col_blocks, col_blocks) for ref in (c_high, c_low))
    total = jnp.zeros((half * width, half * width), jnp.float32)
    total_out[...] = add_products(total, left, r_high, r_low, row_pairs(core, rows_blocks, own, core_own))


def second_kernel(half, width, col_blocks, rows_blocks, scalars, total, r_high, r_low, c_high, c_low, partner, core_partner, out):
    wave_id, core = scalars[scalars.shape[0] - 5 + 1], scalars[scalars.shape[0] - 5 + 2]
    left = tuple(columns(ref, (1 - wave_id) * col_blocks, col_blocks) for ref in (c_high, c_low))
    total = add_products(total[...], left, r_high, r_low, row_pairs(core, rows_blocks, partner, core_partner))
    blocks = [total[s * width : (s + 1) * width, s * width : (s + 1) * width] for s in range(half)]
    for i in range(half // 2):
        out[i] = jnp.concatenate([blocks[i], blocks[i + half // 2]], axis=1)


def put_rows(step, places, sources, col_blocks, a_high, a_low, rows=None):
    for place, source in zip(places, sources):
        for part in range(col_blocks):
            inside = slice(part * BLK, (part + 1) * BLK)
            high, low = split(source[:, inside] if rows is None else source[rows, inside])
            a_high[place * col_blocks + part] = high
            a_low[place * col_blocks + part] = low


def prepare_kernel(n_col, sibs, nbk, col_blocks, scalars, dinv, *refs):
    far = n_col // 2
    normed, own, partner = refs[:2], refs[2], refs[3]
    mine, theirs = refs[4 : 3 + far], refs[3 + far : 2 + 2 * far]
    n_high, n_low, a_high, a_low, base_out = refs[2 + 2 * far :]
    col_id, wave_id, core = scalars[scalars.shape[0] - 5 + 0], scalars[scalars.shape[0] - 5 + 1], scalars[scalars.shape[0] - 5 + 2]
    half = sibs // 2
    for ref, who in zip(normed, (core, 1 - core)):
        for slot in range(nbk):
            high, low = split(ref[slot])
            n_high[slot, pl.ds(who * half, half)] = high
            n_low[slot, pl.ds(who * half, half)] = low
    here = pl.ds(pl.multiple_of(col_id * BLK, BLK), BLK)
    for step in range(far):
        places = [step * 2 + wave_id, step * 2 + 1 - wave_id]
        if step:
            put_rows(step, places, (mine[step - 1], theirs[step - 1]), col_blocks, a_high, a_low)
        else:
            put_rows(step, places, (own, partner), col_blocks, a_high, a_low, here)
    bases = []
    for s in range(sibs):
        factor = split(dinv[s])
        bases.append(packed_product(factor, factor, CONTRACT_FIRST))
    for i in range(half // 2):
        for first in (0, half):
            base_out[first // 2 + i] = jnp.concatenate([bases[first + i], bases[first + half // 2 + i]], axis=1)


def panel_kernel(n_col, sibs, nbk, col_blocks, scalars, n_high, n_low, early_high, early_low, *refs):
    far = n_col // 2
    mine, theirs = refs[: n_col - far], refs[n_col - far : 2 * (n_col - far)]
    panel_out, a_high, a_low, held, sems = refs[2 * (n_col - far) :]
    col_id, wave_id, core, block = scalars[scalars.shape[0] - 5 + 0], scalars[scalars.shape[0] - 5 + 1], scalars[scalars.shape[0] - 5 + 2], scalars[scalars.shape[0] - 5 + 4]
    group = 2 * col_blocks
    for step in range(far):
        for part in range(group):
            a_high[(col_id ^ step) * group + part] = early_high[step * group + part]
            a_low[(col_id ^ step) * group + part] = early_low[step * group + part]
    for i, step in enumerate(range(far, n_col)):
        places = [(col_id ^ step) * 2 + wave_id, (col_id ^ step) * 2 + 1 - wave_id]
        put_rows(step, places, (mine[i], theirs[i]), col_blocks, a_high, a_low)

    def sibling(s, carry):
        total = jnp.zeros((n_high.shape[2], BLK), jnp.float32)
        found = False
        width = min(4, nbk)
        for first in range(0, nbk, width):
            places = [scalars[(s) * nbk + first + k] for k in range(width)]
            left = tuple(jnp.concatenate([ref[first + k, s] for k in range(width)], axis=1) for ref in (n_high, n_low))
            right = tuple(jnp.concatenate([ref[place] for place in places], axis=1) for ref in (a_high, a_low))
            total = total + packed_product(left, right, CONTRACT_LAST)
            for place in places:
                found = jnp.logical_or(found, place == block)
        held[s] = total * jnp.where(found, -1.0, 0.0)
        pltpu.make_async_copy(held.at[s], panel_out.at[s], sems.at[s]).start()
        return carry

    if sibs * nbk <= 64:
        for s in range(sibs):
            sibling(s, 0)
    else:
        lax.fori_loop(0, sibs, sibling, 0)
    for s in range(sibs):
        pltpu.make_async_copy(held.at[s], panel_out.at[s], sems.at[s]).wait()


def per_device(lower_panel, diag_inverse, ancestor_inverse, pattern):
    sibs, width, packed = lower_panel.shape
    rows_here, cols_here = ancestor_inverse.shape
    n_row, n_col = lax.axis_size("row"), lax.axis_size("col")
    row_id, col_id, wave_id = (lax.axis_index(axis) for axis in ("row", "col", "wave"))
    core = row_id % 2
    own_rows = rows_here // n_col
    slots, col_blocks, nbk = packed // BLK, cols_here // BLK, pattern.shape[1]
    rows_blocks = rows_here // BLK
    half, quarter = sibs // 2, sibs // 4
    n_blocks = n_col * 2 * col_blocks
    f32, bf16 = jnp.float32, jnp.bfloat16
    smem = pl.BlockSpec(memory_space=pltpu.SMEM)
    vmem = pl.BlockSpec(memory_space=pltpu.VMEM)
    mib = 2**20
    size = rows_here * cols_here * 4 // mib + 1
    params = pltpu.CompilerParams(vmem_limit_bytes=min(60, 12 + 12 * size) * mib)
    ids = jnp.stack([col_id, wave_id, core, row_id, row_id * n_col + col_id]).astype(jnp.int32)

    def call(kernel, out_shape, operands, scratch, flops, out_space=vmem):
        moved = sum(x.size * 4 for x in operands)
        return pl.pallas_call(
            kernel,
            out_shape=out_shape,
            in_specs=[smem] + [vmem] * len(operands),
            out_specs=jax.tree.map(lambda _: out_space, out_shape),
            scratch_shapes=scratch,
            compiler_params=params,
            cost_estimate=pl.CostEstimate(flops=flops, bytes_accessed=(moved if flops > 10 else 1), transcendentals=0),
        )(scalars, *operands)

    def tie(point, value):
        names = [name for name in late if due(name) == point]
        if names:
            value, *tied = lax.optimization_barrier((value, *[late[name] for name in names]))
            late.update(zip(names, tied))
        return value

    def due(name):
        if name.startswith("prep"):
            return DONE.get("prep")
        if name[-1].isdigit():
            stem = name.rstrip("0123456789")
            return DONE.get(stem + str(min(int(name[len(stem) :]), 2)))
        return DONE.get(name)

    far = n_col // 2
    late = {}
    half_panel = lax.dynamic_slice_in_dim(lower_panel, core * half, half, 0)
    source = ancestor_inverse
    if GATE.get("wave"):
        source, half_panel = lax.optimization_barrier((source, half_panel))
    partner = xor_permute(source, "wave", 1)
    halves = {0: half_panel}
    halves[far] = xor_permute(halves[0], "col", far)
    chunks = [
        lax.dynamic_slice_in_dim(ancestor_inverse, (col_id ^ step) * own_rows, own_rows, 0) for step in range(1, n_col)
    ]
    if GATE.get("slices"):
        half_panel, *chunks = lax.optimization_barrier((half_panel, *chunks))
        halves[0] = half_panel
        halves[far] = xor_permute(half_panel, "col", far)
    gated = [i for i in range(n_col - 1) if GATE.get("mine" + str(min(i, 2))) == 1]
    if gated:
        halves[far], *held = lax.optimization_barrier((halves[far], *[chunks[i] for i in gated]))
        for i, chunk in zip(gated, held):
            chunks[i] = chunk
    held_back = [i for i in range(n_col - 1) if GATE.get("mine" + str(min(i, 2))) == 2]
    for i in range(n_col - 1):
        if i not in held_back:
            late["mine" + str(i)] = xor_permute(chunks[i], "col", i + 1)
            if not TIED:
                late["theirs" + str(i)] = xor_permute(late["mine" + str(i)], "wave", 1)
    late["core_own"] = xor_permute(ancestor_inverse, "row", 1)
    scalars = jnp.concatenate([pattern.reshape(-1), ids])
    if GATE.get("scalars"):
        halves[far], scalars = lax.optimization_barrier((halves[far], scalars))
    halves[far] = tie(0, halves[far])
    halves[far] = call(norm_kernel, jax.ShapeDtypeStruct(half_panel.shape, f32), [diag_inverse, halves[far]], [], 100000000000)
    halves[far] = tie(8, halves[far])
    near = halves[0]
    if GATE.get("near") == 1:
        halves[far], near = lax.optimization_barrier((halves[far], near))
    if GATE.get("near") == 2:
        near, *_ = lax.optimization_barrier((near, *chunks))
    if GATE.get("near") == 3:
        near, late["core_own"] = lax.optimization_barrier((near, late["core_own"]))
    bit = far // 2
    while bit:
        for step in list(halves):
            halves[step ^ bit] = xor_permute(halves[step] if step else near, "col", bit)
        bit //= 2
    if held_back:
        halves[n_col - 1], *held = lax.optimization_barrier((halves[n_col - 1], *[chunks[i] for i in held_back]))
        for i, chunk in zip(held_back, held):
            late["mine" + str(i)] = xor_permute(chunk, "col", i + 1)
            if not TIED:
                late["theirs" + str(i)] = xor_permute(late["mine" + str(i)], "wave", 1)
    partner, *tied = lax.optimization_barrier((partner, *[halves[step] for step in range(n_col)]))
    halves = dict(enumerate(tied))
    partner = tie(1, partner)
    core_partner = xor_permute(partner, "row", 1)
    if SPLIT:
        square = half * width
        partial, normed, *placed = call(
            functools.partial(first_kernel, n_col, slots, col_blocks, rows_blocks),
            (
                jax.ShapeDtypeStruct((square, square), f32),
                jax.ShapeDtypeStruct((nbk, half, width, BLK), f32),
                jax.ShapeDtypeStruct((2 * rows_blocks + 1, square, BLK), bf16),
                jax.ShapeDtypeStruct((2 * rows_blocks + 1, square, BLK), bf16),
                jax.ShapeDtypeStruct((2 * col_blocks + 1, square, BLK), bf16),
                jax.ShapeDtypeStruct((2 * col_blocks + 1, square, BLK), bf16),
            ),
            [diag_inverse] + [halves[step] for step in range(n_col)] + [ancestor_inverse, late["core_own"]],
            [],
            COST[0],
        )
        late["normed_other"] = xor_permute(normed, "row", 1)
        core_partner = tie(2, core_partner)
        total = call(
            functools.partial(second_kernel, half, width, col_blocks, rows_blocks),
            jax.ShapeDtypeStruct((quarter, width, 2 * width), f32),
            [partial, *placed, partner, core_partner],
            [],
            COST[2],
        )
    else:
        core_partner = tie(2, core_partner)
        total, normed = call(
            functools.partial(update_kernel, n_col, slots, col_blocks, rows_blocks),
            (
                jax.ShapeDtypeStruct((quarter, width, 2 * width), f32),
                jax.ShapeDtypeStruct((nbk, half, width, BLK), f32),
            ),
            [diag_inverse] + [halves[step] for step in range(n_col)]
            + [ancestor_inverse, partner, late["core_own"], core_partner],
            [pltpu.VMEM((2 * rows_blocks + 1, half * width, BLK), bf16)] * 2
            + [pltpu.VMEM((2 * col_blocks + 1, half * width, BLK), bf16)] * 2,
            COST[0],
        )
        late["normed_other"] = xor_permute(normed, "row", 1)
    total = tie(3, total)
    bits = [2**i for i in range(1, n_row.bit_length() - 1)]
    if RADIX:
        last = bits.pop()
    for bit in bits:
        total = total + xor_permute(total, "row", bit)
    total = tie(4, total)
    early = [diag_inverse, normed, late["normed_other"], ancestor_inverse, partner]
    early += [late[name + str(i)] for name in ("mine", "theirs") for i in range(far - 1)]
    prepared = call(
        functools.partial(prepare_kernel, n_col, sibs, nbk, col_blocks),
        (
            jax.ShapeDtypeStruct((nbk, sibs, width, BLK), bf16),
            jax.ShapeDtypeStruct((nbk, sibs, width, BLK), bf16),
            jax.ShapeDtypeStruct((n_blocks // 2, BLK, BLK), bf16),
            jax.ShapeDtypeStruct((n_blocks // 2, BLK, BLK), bf16),
            jax.ShapeDtypeStruct((half, width, 2 * width), f32),
        ),
        early,
        [],
        COST[3] if len(COST) > 3 else 10**7,
    )
    late.update({"prep" + str(i): x for i, x in enumerate(prepared)})
    bits = [2**i for i in range(n_col.bit_length() - 1)]
    if RADIX:
        first = bits.pop(0)
        both = [(r * n_col + c, (r ^ last) * n_col + (c ^ first)) for r in range(n_row) for c in range(n_col)]
        steps = [
            xor_permute(total, "row", last),
            xor_permute(total, "col", first),
            lax.ppermute(total, ("row", "col"), both),
        ]
        total = (total + steps[0]) + (steps[1] + steps[2])
        total = tie(5, total)
    for i, bit in enumerate(bits):
        if MIX:
            turn = (bit, bits[len(bits) - 1 - i])
            pairs = [(r * n_col + c, r * n_col + (c ^ turn[r % 2])) for r in range(n_row) for c in range(n_col)]
            total = total + lax.ppermute(total, ("row", "col"), pairs)
        else:
            total = total + xor_permute(total, "col", bit)
        if i == 0 and not RADIX:
            total = tie(5, total)
    total = tie(6, total)
    panel = call(
        functools.partial(panel_kernel, n_col, sibs, nbk, col_blocks),
        jax.ShapeDtypeStruct((sibs, width, BLK), f32),
        [late["prep" + str(i)] for i in range(4)]
        + [late[name + str(i)] for name in ("mine", "theirs") for i in range(far - 1, n_col - 1)],
        [
            pltpu.VMEM((n_blocks, BLK, BLK), bf16),
            pltpu.VMEM((n_blocks, BLK, BLK), bf16),
            pltpu.VMEM((sibs, width, BLK), f32),
            pltpu.SemaphoreType.DMA((sibs,)),
        ],
        COST[1],
        pl.BlockSpec(memory_space=pl.ANY),
    )
    base = late["prep4"]
    if DONE.get("panel") == 6:
        total, panel = lax.optimization_barrier((total, panel))
    other = xor_permute(total, "row", 1)
    if DONE.get("panel") == 7:
        other, panel = lax.optimization_barrier((other, panel))
    first = jnp.where(core == 0, total, other) + base[:quarter]
    second = jnp.where(core == 0, other, total) + base[quarter:]
    diag = jnp.concatenate([first[..., :width], first[..., width:], second[..., :width], second[..., width:]], axis=0)
    return panel, diag


def solution(mesh):
    return jax.shard_map(
        per_device,
        mesh=mesh,
        in_specs=(
            P("wave", None, "col"),
            P("wave", None, None),
            P("row", ("col", "wave")),
            P("wave", None),
        ),
        out_specs=(P("wave", None, ("row", "col")), P("wave", None, None)),
        check_vma=False,
    )
```

```python
import functools

import jax
import jax.numpy as jnp
from jax import lax
from jax.experimental import pallas as pl
from jax.experimental.pallas import tpu as pltpu
from jax.sharding import PartitionSpec as P

BLK = 128
CONTRACT_LAST = ((1,), (1,))
CONTRACT_FIRST = ((0,), (0,))


DONE = {'core_own': 2, 'mine0': 2, 'mine1': 5, 'mine2': 3, 'normed_other': 4, 'panel': 6, 'prep': None, 'theirs0': 5, 'theirs1': None, 'theirs2': None}
GATE = {'mine0': 0, 'mine2': False, 'scalars': True}
SPLIT = True
RADIX = False
MIX = False
TIED = False
COST = [100000000000, 100000000000, 100000000000]


def xor_permute(value, axis, distance):
    return lax.ppermute(value, axis, [(i, i ^ distance) for i in range(lax.axis_size(axis))])


def split(value):
    high = value.astype(jnp.bfloat16)
    return high, (value - high.astype(jnp.float32)).astype(jnp.bfloat16)


def product(left, right, dims):
    dot = functools.partial(lax.dot_general, dimension_numbers=(dims, ((), ())), preferred_element_type=jnp.float32)
    return dot(left[0], right[0]) + (dot(left[0], right[1]) + dot(left[1], right[0]))


def norm_kernel(scalars, dinv, lower, out):
    half = out.shape[0]
    core = scalars[scalars.shape[0] - 3]
    for s in range(half):
        out[s] = packed_product(split(dinv[core * half + s]), split(lower[s]), CONTRACT_FIRST)


def packed_product(left, right, dims):
    axis = 1 - dims[0][0]
    rows, columns = left[0].shape[axis], right[0].shape[axis]
    both = lax.dot_general(
        jnp.concatenate(left, axis=axis),
        jnp.concatenate(right, axis=axis),
        (dims, ((), ())),
        preferred_element_type=jnp.float32,
    )
    return both[:rows, :columns] + (both[:rows, columns:] + both[rows:, :columns])


def update_kernel(n_col, slots, col_blocks, rows_blocks, scalars, dinv, *refs):
    halves, (own, partner, core_own, core_partner) = refs[:n_col], refs[n_col : n_col + 4]
    out, normed_out, r_high, r_low, c_high, c_low = refs[n_col + 4 :]
    nbk = n_col * slots
    col_id, wave_id, core, row_id = scalars[scalars.shape[0] - 5 + 0], scalars[scalars.shape[0] - 5 + 1], scalars[scalars.shape[0] - 5 + 2], scalars[scalars.shape[0] - 5 + 3]
    half, width = halves[0].shape[0], halves[0].shape[1]
    row_first = (row_id - core) * rows_blocks
    col_first = col_id * 2 * col_blocks
    n_rows, n_cols = 2 * rows_blocks, 2 * col_blocks
    for ref in (r_high, r_low, c_high, c_low):
        ref[...] = jnp.zeros_like(ref)
    for s in range(half):
        far = n_col // 2
        lower = jnp.concatenate([halves[step][s] for step in range(far)], axis=1)
        normed = packed_product(split(dinv[core * half + s]), split(lower), CONTRACT_FIRST)
        normed = jnp.concatenate([normed] + [halves[step][s] for step in range(far, n_col)], axis=1)
        for step in range(n_col):
            for slot in range(slots):
                first = (step * slots + slot) * BLK
                here = normed[:, first : first + BLK]
                number = (col_id ^ step) * slots + slot
                normed_out[number, s] = here
                high, low = split(here)
                place = scalars[(core * half + s) * nbk + number]
                for first, count, to_high, to_low in ((row_first, n_rows, r_high, r_low), (col_first, n_cols, c_high, c_low)):
                    inside = jnp.logical_and(place >= first, place < first + count)
                    target = jnp.where(inside, place - first, count)
                    to_high[target, s * width : (s + 1) * width] = high
                    to_low[target, s * width : (s + 1) * width] = low

    def columns(ref):
        mine = [ref[wave_id * col_blocks + part] for part in range(col_blocks)]
        theirs = [ref[(1 - wave_id) * col_blocks + part] for part in range(col_blocks)]
        return jnp.concatenate(mine + theirs, axis=1)

    left = columns(c_high), columns(c_low)
    total = jnp.zeros((half * width, half * width), jnp.float32)
    group = 2
    for who, mine, theirs in ((core, own, partner), (1 - core, core_own, core_partner)):
        for first in range(0, rows_blocks, group):
            rows = slice(first * BLK, (first + group) * BLK)
            block = split(jnp.concatenate([mine[rows, :], theirs[rows, :]], axis=1))
            part = product(left, block, CONTRACT_LAST)
            place = who * rows_blocks + first
            right = tuple(jnp.concatenate([ref[place + i] for i in range(group)], axis=1) for ref in (r_high, r_low))
            total = total + product(right, split(part), CONTRACT_LAST)
    blocks = [total[s * width : (s + 1) * width, s * width : (s + 1) * width] for s in range(half)]
    for i in range(half // 2):
        out[i] = jnp.concatenate([blocks[i], blocks[i + half // 2]], axis=1)


def add_products(total, left, r_high, r_low, blocks):
    for place, rows in blocks:
        part = product(left, split(rows), CONTRACT_LAST)
        right = tuple(jnp.concatenate([ref[place], ref[place + 1]], axis=1) for ref in (r_high, r_low))
        total = total + product(right, split(part), CONTRACT_LAST)
    return total


def row_pairs(core, rows_blocks, own, other):
    for who, ref in ((core, own), (1 - core, other)):
        for first in range(0, rows_blocks, 2):
            yield who * rows_blocks + first, ref[first * BLK : (first + 2) * BLK, :]


def columns(ref, first, count):
    return jnp.concatenate([ref[first + part] for part in range(count)], axis=1)


def first_kernel(n_col, slots, col_blocks, rows_blocks, scalars, dinv, *refs):
    halves, own, core_own = refs[:n_col], refs[n_col], refs[n_col + 1]
    total_out, normed_out, r_high, r_low, c_high, c_low = refs[n_col + 2 :]
    nbk = n_col * slots
    col_id, wave_id, core, row_id = scalars[scalars.shape[0] - 5 + 0], scalars[scalars.shape[0] - 5 + 1], scalars[scalars.shape[0] - 5 + 2], scalars[scalars.shape[0] - 5 + 3]
    half, width = halves[0].shape[0], halves[0].shape[1]
    row_first = (row_id - core) * rows_blocks
    col_first = col_id * 2 * col_blocks
    n_rows, n_cols = 2 * rows_blocks, 2 * col_blocks
    for ref in (r_high, r_low, c_high, c_low):
        ref[...] = jnp.zeros_like(ref)
    for s in range(half):
        far = n_col // 2
        lower = jnp.concatenate([halves[step][s] for step in range(far)], axis=1)
        normed = packed_product(split(dinv[core * half + s]), split(lower), CONTRACT_FIRST)
        normed = jnp.concatenate([normed] + [halves[step][s] for step in range(far, n_col)], axis=1)
        for step in range(n_col):
            for slot in range(slots):
                first = (step * slots + slot) * BLK
                here = normed[:, first : first + BLK]
                number = (col_id ^ step) * slots + slot
                normed_out[number, s] = here
                high, low = split(here)
                place = scalars[(core * half + s) * nbk + number]
                for first, count, to_high, to_low in ((row_first, n_rows, r_high, r_low), (col_first, n_cols, c_high, c_low)):
                    inside = jnp.logical_and(place >= first, place < first + count)
                    target = jnp.where(inside, place - first, count)
                    to_high[target, s * width : (s + 1) * width] = high
                    to_low[target, s * width : (s + 1) * width] = low
    left = tuple(columns(ref, wave_id * col_blocks, col_blocks) for ref in (c_high, c_low))
    total = jnp.zeros((half * width, half * width), jnp.float32)
    total_out[...] = add_products(total, left, r_high, r_low, row_pairs(core, rows_blocks, own, core_own))


def second_kernel(half, width, col_blocks, rows_blocks, scalars, total, r_high, r_low, c_high, c_low, partner, core_partner, out):
    wave_id, core = scalars[scalars.shape[0] - 5 + 1], scalars[scalars.shape[0] - 5 + 2]
    left = tuple(columns(ref, (1 - wave_id) * col_blocks, col_blocks) for ref in (c_high, c_low))
    total = add_products(total[...], left, r_high, r_low, row_pairs(core, rows_blocks, partner, core_partner))
    blocks = [total[s * width : (s + 1) * width, s * width : (s + 1) * width] for s in range(half)]
    for i in range(half // 2):
        out[i] = jnp.concatenate([blocks[i], blocks[i + half // 2]], axis=1)


def put_rows(step, places, sources, col_blocks, a_high, a_low, rows=None):
    for place, source in zip(places, sources):
        for part in range(col_blocks):
            inside = slice(part * BLK, (part + 1) * BLK)
            high, low = split(source[:, inside] if rows is None else source[rows, inside])
            a_high[place * col_blocks + part] = high
            a_low[place * col_blocks + part] = low


def prepare_kernel(n_col, sibs, nbk, col_blocks, scalars, dinv, *refs):
    far = n_col // 2
    normed, own, partner = refs[:2], refs[2], refs[3]
    mine, theirs = refs[4 : 3 + far], refs[3 + far : 2 + 2 * far]
    n_high, n_low, a_high, a_low, base_out = refs[2 + 2 * far :]
    col_id, wave_id, core = scalars[scalars.shape[0] - 5 + 0], scalars[scalars.shape[0] - 5 + 1], scalars[scalars.shape[0] - 5 + 2]
    half = sibs // 2
    for ref, who in zip(normed, (core, 1 - core)):
        for slot in range(nbk):
            high, low = split(ref[slot])
            n_high[slot, pl.ds(who * half, half)] = high
            n_low[slot, pl.ds(who * half, half)] = low
    here = pl.ds(pl.multiple_of(col_id * BLK, BLK), BLK)
    for step in range(far):
        places = [step * 2 + wave_id, step * 2 + 1 - wave_id]
        if step:
            put_rows(step, places, (mine[step - 1], theirs[step - 1]), col_blocks, a_high, a_low)
        else:
            put_rows(step, places, (own, partner), col_blocks, a_high, a_low, here)
    bases = []
    for s in range(sibs):
        factor = split(dinv[s])
        bases.append(packed_product(factor, factor, CONTRACT_FIRST))
    for i in range(half // 2):
        for first in (0, half):
            base_out[first // 2 + i] = jnp.concatenate([bases[first + i], bases[first + half // 2 + i]], axis=1)


def panel_kernel(n_col, sibs, nbk, col_blocks, scalars, n_high, n_low, early_high, early_low, *refs):
    far = n_col // 2
    mine, theirs = refs[: n_col - far], refs[n_col - far : 2 * (n_col - far)]
    panel_out, a_high, a_low, held, sems = refs[2 * (n_col - far) :]
    col_id, wave_id, core, block = scalars[scalars.shape[0] - 5 + 0], scalars[scalars.shape[0] - 5 + 1], scalars[scalars.shape[0] - 5 + 2], scalars[scalars.shape[0] - 5 + 4]
    group = 2 * col_blocks
    for step in range(far):
        for part in range(group):
            a_high[(col_id ^ step) * group + part] = early_high[step * group + part]
            a_low[(col_id ^ step) * group + part] = early_low[step * group + part]
    for i, step in enumerate(range(far, n_col)):
        places = [(col_id ^ step) * 2 + wave_id, (col_id ^ step) * 2 + 1 - wave_id]
        put_rows(step, places, (mine[i], theirs[i]), col_blocks, a_high, a_low)

    def sibling(s, carry):
        total = jnp.zeros((n_high.shape[2], BLK), jnp.float32)
        found = False
        width = min(4, nbk)
        for first in range(0, nbk, width):
            places = [scalars[(s) * nbk + first + k] for k in range(width)]
            left = tuple(jnp.concatenate([ref[first + k, s] for k in range(width)], axis=1) for ref in (n_high, n_low))
            right = tuple(jnp.concatenate([ref[place] for place in places], axis=1) for ref in (a_high, a_low))
            total = total + packed_product(left, right, CONTRACT_LAST)
            for place in places:
                found = jnp.logical_or(found, place == block)
        held[s] = total * jnp.where(found, -1.0, 0.0)
        pltpu.make_async_copy(held.at[s], panel_out.at[s], sems.at[s]).start()
        return carry

    if sibs * nbk <= 64:
        for s in range(sibs):
            sibling(s, 0)
    else:
        lax.fori_loop(0, sibs, sibling, 0)
    for s in range(sibs):
        pltpu.make_async_copy(held.at[s], panel_out.at[s], sems.at[s]).wait()


def per_device(lower_panel, diag_inverse, ancestor_inverse, pattern):
    sibs, width, packed = lower_panel.shape
    rows_here, cols_here = ancestor_inverse.shape
    n_row, n_col = lax.axis_size("row"), lax.axis_size("col")
    row_id, col_id, wave_id = (lax.axis_index(axis) for axis in ("row", "col", "wave"))
    core = row_id % 2
    own_rows = rows_here // n_col
    slots, col_blocks, nbk = packed // BLK, cols_here // BLK, pattern.shape[1]
    rows_blocks = rows_here // BLK
    half, quarter = sibs // 2, sibs // 4
    n_blocks = n_col * 2 * col_blocks
    f32, bf16 = jnp.float32, jnp.bfloat16
    smem = pl.BlockSpec(memory_space=pltpu.SMEM)
    vmem = pl.BlockSpec(memory_space=pltpu.VMEM)
    mib = 2**20
    size = rows_here * cols_here * 4 // mib + 1
    params = pltpu.CompilerParams(vmem_limit_bytes=min(60, 12 + 12 * size) * mib)
    ids = jnp.stack([col_id, wave_id, core, row_id, row_id * n_col + col_id]).astype(jnp.int32)

    def call(kernel, out_shape, operands, scratch, flops, out_space=vmem):
        moved = sum(x.size * 4 for x in operands)
        return pl.pallas_call(
            kernel,
            out_shape=out_shape,
            in_specs=[smem] + [vmem] * len(operands),
            out_specs=jax.tree.map(lambda _: out_space, out_shape),
            scratch_shapes=scratch,
            compiler_params=params,
            cost_estimate=pl.CostEstimate(flops=flops, bytes_accessed=(moved if flops > 10 else 1), transcendentals=0),
        )(scalars, *operands)

    def tie(point, value):
        names = [name for name in late if due(name) == point]
        if names:
            value, *tied = lax.optimization_barrier((value, *[late[name] for name in names]))
            late.update(zip(names, tied))
        return value

    def due(name):
        if name.startswith("prep"):
            return DONE.get("prep")
        if name[-1].isdigit():
            stem = name.rstrip("0123456789")
            return DONE.get(stem + str(min(int(name[len(stem) :]), 2)))
        return DONE.get(name)

    far = n_col // 2
    late = {}
    half_panel = lax.dynamic_slice_in_dim(lower_panel, core * half, half, 0)
    source = ancestor_inverse
    if GATE.get("wave"):
        source, half_panel = lax.optimization_barrier((source, half_panel))
    partner = xor_permute(source, "wave", 1)
    halves = {0: half_panel}
    halves[far] = xor_permute(halves[0], "col", far)
    chunks = [
        lax.dynamic_slice_in_dim(ancestor_inverse, (col_id ^ step) * own_rows, own_rows, 0) for step in range(1, n_col)
    ]
    if GATE.get("slices"):
        half_panel, *chunks = lax.optimization_barrier((half_panel, *chunks))
        halves[0] = half_panel
        halves[far] = xor_permute(half_panel, "col", far)
    gated = [i for i in range(n_col - 1) if GATE.get("mine" + str(min(i, 2))) == 1]
    if gated:
        halves[far], *held = lax.optimization_barrier((halves[far], *[chunks[i] for i in gated]))
        for i, chunk in zip(gated, held):
            chunks[i] = chunk
    held_back = [i for i in range(n_col - 1) if GATE.get("mine" + str(min(i, 2))) == 2]
    for i in range(n_col - 1):
        if i not in held_back:
            late["mine" + str(i)] = xor_permute(chunks[i], "col", i + 1)
            if not TIED:
                late["theirs" + str(i)] = xor_permute(late["mine" + str(i)], "wave", 1)
    late["core_own"] = xor_permute(ancestor_inverse, "row", 1)
    scalars = jnp.concatenate([pattern.reshape(-1), ids])
    if GATE.get("scalars"):
        halves[far], scalars = lax.optimization_barrier((halves[far], scalars))
    halves[far] = tie(0, halves[far])
    halves[far] = call(norm_kernel, jax.ShapeDtypeStruct(half_panel.shape, f32), [diag_inverse, halves[far]], [], 100000000000)
    halves[far] = tie(8, halves[far])
    near = halves[0]
    if GATE.get("near") == 1:
        halves[far], near = lax.optimization_barrier((halves[far], near))
    if GATE.get("near") == 2:
        near, *_ = lax.optimization_barrier((near, *chunks))
    if GATE.get("near") == 3:
        near, late["core_own"] = lax.optimization_barrier((near, late["core_own"]))
    bit = far // 2
    while bit:
        for step in list(halves):
            halves[step ^ bit] = xor_permute(halves[step] if step else near, "col", bit)
        bit //= 2
    if held_back:
        halves[n_col - 1], *held = lax.optimization_barrier((halves[n_col - 1], *[chunks[i] for i in held_back]))
        for i, chunk in zip(held_back, held):
            late["mine" + str(i)] = xor_permute(chunk, "col", i + 1)
            if not TIED:
                late["theirs" + str(i)] = xor_permute(late["mine" + str(i)], "wave", 1)
    partner, *tied = lax.optimization_barrier((partner, *[halves[step] for step in range(n_col)]))
    halves = dict(enumerate(tied))
    partner = tie(1, partner)
    core_partner = xor_permute(partner, "row", 1)
    if SPLIT:
        square = half * width
        partial, normed, *placed = call(
            functools.partial(first_kernel, n_col, slots, col_blocks, rows_blocks),
            (
                jax.ShapeDtypeStruct((square, square), f32),
                jax.ShapeDtypeStruct((nbk, half, width, BLK), f32),
                jax.ShapeDtypeStruct((2 * rows_blocks + 1, square, BLK), bf16),
                jax.ShapeDtypeStruct((2 * rows_blocks + 1, square, BLK), bf16),
                jax.ShapeDtypeStruct((2 * col_blocks + 1, square, BLK), bf16),
                jax.ShapeDtypeStruct((2 * col_blocks + 1, square, BLK), bf16),
            ),
            [diag_inverse] + [halves[step] for step in range(n_col)] + [ancestor_inverse, late["core_own"]],
            [],
            COST[0],
        )
        late["normed_other"] = xor_permute(normed, "row", 1)
        core_partner = tie(2, core_partner)
        total = call(
            functools.partial(second_kernel, half, width, col_blocks, rows_blocks),
            jax.ShapeDtypeStruct((quarter, width, 2 * width), f32),
            [partial, *placed, partner, core_partner],
            [],
            COST[2],
        )
    else:
        core_partner = tie(2, core_partner)
        total, normed = call(
            functools.partial(update_kernel, n_col, slots, col_blocks, rows_blocks),
            (
                jax.ShapeDtypeStruct((quarter, width, 2 * width), f32),
                jax.ShapeDtypeStruct((nbk, half, width, BLK), f32),
            ),
            [diag_inverse] + [halves[step] for step in range(n_col)]
            + [ancestor_inverse, partner, late["core_own"], core_partner],
            [pltpu.VMEM((2 * rows_blocks + 1, half * width, BLK), bf16)] * 2
            + [pltpu.VMEM((2 * col_blocks + 1, half * width, BLK), bf16)] * 2,
            COST[0],
        )
        late["normed_other"] = xor_permute(normed, "row", 1)
    total = tie(3, total)
    bits = [2**i for i in range(1, n_row.bit_length() - 1)]
    if RADIX:
        last = bits.pop()
    for bit in bits:
        total = total + xor_permute(total, "row", bit)
    total = tie(4, total)
    early = [diag_inverse, normed, late["normed_other"], ancestor_inverse, partner]
    early += [late[name + str(i)] for name in ("mine", "theirs") for i in range(far - 1)]
    prepared = call(
        functools.partial(prepare_kernel, n_col, sibs, nbk, col_blocks),
        (
            jax.ShapeDtypeStruct((nbk, sibs, width, BLK), bf16),
            jax.ShapeDtypeStruct((nbk, sibs, width, BLK), bf16),
            jax.ShapeDtypeStruct((n_blocks // 2, BLK, BLK), bf16),
            jax.ShapeDtypeStruct((n_blocks // 2, BLK, BLK), bf16),
            jax.ShapeDtypeStruct((half, width, 2 * width), f32),
        ),
        early,
        [],
        COST[3] if len(COST) > 3 else 10**7,
    )
    late.update({"prep" + str(i): x for i, x in enumerate(prepared)})
    bits = [2**i for i in range(n_col.bit_length() - 1)]
    if RADIX:
        first = bits.pop(0)
        both = [(r * n_col + c, (r ^ last) * n_col + (c ^ first)) for r in range(n_row) for c in range(n_col)]
        steps = [
            xor_permute(total, "row", last),
            xor_permute(total, "col", first),
            lax.ppermute(total, ("row", "col"), both),
        ]
        total = (total + steps[0]) + (steps[1] + steps[2])
        total = tie(5, total)
    for i, bit in enumerate(bits):
        if MIX:
            turn = (bit, bits[len(bits) - 1 - i])
            pairs = [(r * n_col + c, r * n_col + (c ^ turn[r % 2])) for r in range(n_row) for c in range(n_col)]
            total = total + lax.ppermute(total, ("row", "col"), pairs)
        else:
            total = total + xor_permute(total, "col", bit)
        if i == 0 and not RADIX:
            total = tie(5, total)
    total = tie(6, total)
    panel = call(
        functools.partial(panel_kernel, n_col, sibs, nbk, col_blocks),
        jax.ShapeDtypeStruct((sibs, width, BLK), f32),
        [late["prep" + str(i)] for i in range(4)]
        + [late[name + str(i)] for name in ("mine", "theirs") for i in range(far - 1, n_col - 1)],
        [
            pltpu.VMEM((n_blocks, BLK, BLK), bf16),
            pltpu.VMEM((n_blocks, BLK, BLK), bf16),
            pltpu.VMEM((sibs, width, BLK), f32),
            pltpu.SemaphoreType.DMA((sibs,)),
        ],
        COST[1],
        pl.BlockSpec(memory_space=pl.ANY),
    )
    base = late["prep4"]
    if DONE.get("panel") == 6:
        total, panel = lax.optimization_barrier((total, panel))
    other = xor_permute(total, "row", 1)
    if DONE.get("panel") == 7:
        other, panel = lax.optimization_barrier((other, panel))
    first = jnp.where(core == 0, total, other) + base[:quarter]
    second = jnp.where(core == 0, other, total) + base[quarter:]
    diag = jnp.concatenate([first[..., :width], first[..., width:], second[..., :width], second[..., width:]], axis=0)
    return panel, diag


def solution(mesh):
    return jax.shard_map(
        per_device,
        mesh=mesh,
        in_specs=(
            P("wave", None, "col"),
            P("wave", None, None),
            P("row", ("col", "wave")),
            P("wave", None),
        ),
        out_specs=(P("wave", None, ("row", "col")), P("wave", None, None)),
        check_vma=False,
    )
```

```python
import functools

import jax
import jax.numpy as jnp
from jax import lax
from jax.experimental import pallas as pl
from jax.experimental.pallas import tpu as pltpu
from jax.sharding import PartitionSpec as P

BLK = 128
CONTRACT_LAST = ((1,), (1,))
CONTRACT_FIRST = ((0,), (0,))


DONE = {'core_own': 2, 'mine0': 2, 'mine1': 5, 'mine2': 3, 'normed_other': 4, 'panel': 6, 'prep': 4, 'theirs0': 5, 'theirs1': None, 'theirs2': None}
GATE = {'mine0': 0, 'mine2': False, 'scalars': True}
SPLIT = True
RADIX = True
MIX = False
TIED = False
COST = [100000000000, 100000000000, 100000000000]


def xor_permute(value, axis, distance):
    return lax.ppermute(value, axis, [(i, i ^ distance) for i in range(lax.axis_size(axis))])


def split(value):
    high = value.astype(jnp.bfloat16)
    return high, (value - high.astype(jnp.float32)).astype(jnp.bfloat16)


def product(left, right, dims):
    dot = functools.partial(lax.dot_general, dimension_numbers=(dims, ((), ())), preferred_element_type=jnp.float32)
    return dot(left[0], right[0]) + (dot(left[0], right[1]) + dot(left[1], right[0]))


def norm_kernel(scalars, dinv, lower, out):
    half = out.shape[0]
    core = scalars[scalars.shape[0] - 3]
    for s in range(half):
        out[s] = packed_product(split(dinv[core * half + s]), split(lower[s]), CONTRACT_FIRST)


def packed_product(left, right, dims):
    axis = 1 - dims[0][0]
    rows, columns = left[0].shape[axis], right[0].shape[axis]
    both = lax.dot_general(
        jnp.concatenate(left, axis=axis),
        jnp.concatenate(right, axis=axis),
        (dims, ((), ())),
        preferred_element_type=jnp.float32,
    )
    return both[:rows, :columns] + (both[:rows, columns:] + both[rows:, :columns])


def update_kernel(n_col, slots, col_blocks, rows_blocks, scalars, dinv, *refs):
    halves, (own, partner, core_own, core_partner) = refs[:n_col], refs[n_col : n_col + 4]
    out, normed_out, r_high, r_low, c_high, c_low = refs[n_col + 4 :]
    nbk = n_col * slots
    col_id, wave_id, core, row_id = scalars[scalars.shape[0] - 5 + 0], scalars[scalars.shape[0] - 5 + 1], scalars[scalars.shape[0] - 5 + 2], scalars[scalars.shape[0] - 5 + 3]
    half, width = halves[0].shape[0], halves[0].shape[1]
    row_first = (row_id - core) * rows_blocks
    col_first = col_id * 2 * col_blocks
    n_rows, n_cols = 2 * rows_blocks, 2 * col_blocks
    for ref in (r_high, r_low, c_high, c_low):
        ref[...] = jnp.zeros_like(ref)
    for s in range(half):
        far = n_col // 2
        lower = jnp.concatenate([halves[step][s] for step in range(far)], axis=1)
        normed = packed_product(split(dinv[core * half + s]), split(lower), CONTRACT_FIRST)
        normed = jnp.concatenate([normed] + [halves[step][s] for step in range(far, n_col)], axis=1)
        for step in range(n_col):
            for slot in range(slots):
                first = (step * slots + slot) * BLK
                here = normed[:, first : first + BLK]
                number = (col_id ^ step) * slots + slot
                normed_out[number, s] = here
                high, low = split(here)
                place = scalars[(core * half + s) * nbk + number]
                for first, count, to_high, to_low in ((row_first, n_rows, r_high, r_low), (col_first, n_cols, c_high, c_low)):
                    inside = jnp.logical_and(place >= first, place < first + count)
                    target = jnp.where(inside, place - first, count)
                    to_high[target, s * width : (s + 1) * width] = high
                    to_low[target, s * width : (s + 1) * width] = low

    def columns(ref):
        mine = [ref[wave_id * col_blocks + part] for part in range(col_blocks)]
        theirs = [ref[(1 - wave_id) * col_blocks + part] for part in range(col_blocks)]
        return jnp.concatenate(mine + theirs, axis=1)

    left = columns(c_high), columns(c_low)
    total = jnp.zeros((half * width, half * width), jnp.float32)
    group = 2
    for who, mine, theirs in ((core, own, partner), (1 - core, core_own, core_partner)):
        for first in range(0, rows_blocks, group):
            rows = slice(first * BLK, (first + group) * BLK)
            block = split(jnp.concatenate([mine[rows, :], theirs[rows, :]], axis=1))
            part = product(left, block, CONTRACT_LAST)
            place = who * rows_blocks + first
            right = tuple(jnp.concatenate([ref[place + i] for i in range(group)], axis=1) for ref in (r_high, r_low))
            total = total + product(right, split(part), CONTRACT_LAST)
    blocks = [total[s * width : (s + 1) * width, s * width : (s + 1) * width] for s in range(half)]
    for i in range(half // 2):
        out[i] = jnp.concatenate([blocks[i], blocks[i + half // 2]], axis=1)


def add_products(total, left, r_high, r_low, blocks):
    for place, rows in blocks:
        part = product(left, split(rows), CONTRACT_LAST)
        right = tuple(jnp.concatenate([ref[place], ref[place + 1]], axis=1) for ref in (r_high, r_low))
        total = total + product(right, split(part), CONTRACT_LAST)
    return total


def row_pairs(core, rows_blocks, own, other):
    for who, ref in ((core, own), (1 - core, other)):
        for first in range(0, rows_blocks, 2):
            yield who * rows_blocks + first, ref[first * BLK : (first + 2) * BLK, :]


def columns(ref, first, count):
    return jnp.concatenate([ref[first + part] for part in range(count)], axis=1)


def first_kernel(n_col, slots, col_blocks, rows_blocks, scalars, dinv, *refs):
    halves, own, core_own = refs[:n_col], refs[n_col], refs[n_col + 1]
    total_out, normed_out, r_high, r_low, c_high, c_low = refs[n_col + 2 :]
    nbk = n_col * slots
    col_id, wave_id, core, row_id = scalars[scalars.shape[0] - 5 + 0], scalars[scalars.shape[0] - 5 + 1], scalars[scalars.shape[0] - 5 + 2], scalars[scalars.shape[0] - 5 + 3]
    half, width = halves[0].shape[0], halves[0].shape[1]
    row_first = (row_id - core) * rows_blocks
    col_first = col_id * 2 * col_blocks
    n_rows, n_cols = 2 * rows_blocks, 2 * col_blocks
    for ref in (r_high, r_low, c_high, c_low):
        ref[...] = jnp.zeros_like(ref)
    for s in range(half):
        far = n_col // 2
        lower = jnp.concatenate([halves[step][s] for step in range(far)], axis=1)
        normed = packed_product(split(dinv[core * half + s]), split(lower), CONTRACT_FIRST)
        normed = jnp.concatenate([normed] + [halves[step][s] for step in range(far, n_col)], axis=1)
        for step in range(n_col):
            for slot in range(slots):
                first = (step * slots + slot) * BLK
                here = normed[:, first : first + BLK]
                number = (col_id ^ step) * slots + slot
                normed_out[number, s] = here
                high, low = split(here)
                place = scalars[(core * half + s) * nbk + number]
                for first, count, to_high, to_low in ((row_first, n_rows, r_high, r_low), (col_first, n_cols, c_high, c_low)):
                    inside = jnp.logical_and(place >= first, place < first + count)
                    target = jnp.where(inside, place - first, count)
                    to_high[target, s * width : (s + 1) * width] = high
                    to_low[target, s * width : (s + 1) * width] = low
    left = tuple(columns(ref, wave_id * col_blocks, col_blocks) for ref in (c_high, c_low))
    total = jnp.zeros((half * width, half * width), jnp.float32)
    total_out[...] = add_products(total, left, r_high, r_low, row_pairs(core, rows_blocks, own, core_own))


def second_kernel(half, width, col_blocks, rows_blocks, scalars, total, r_high, r_low, c_high, c_low, partner, core_partner, out):
    wave_id, core = scalars[scalars.shape[0] - 5 + 1], scalars[scalars.shape[0] - 5 + 2]
    left = tuple(columns(ref, (1 - wave_id) * col_blocks, col_blocks) for ref in (c_high, c_low))
    total = add_products(total[...], left, r_high, r_low, row_pairs(core, rows_blocks, partner, core_partner))
    blocks = [total[s * width : (s + 1) * width, s * width : (s + 1) * width] for s in range(half)]
    for i in range(half // 2):
        out[i] = jnp.concatenate([blocks[i], blocks[i + half // 2]], axis=1)


def put_rows(step, places, sources, col_blocks, a_high, a_low, rows=None):
    for place, source in zip(places, sources):
        for part in range(col_blocks):
            inside = slice(part * BLK, (part + 1) * BLK)
            high, low = split(source[:, inside] if rows is None else source[rows, inside])
            a_high[place * col_blocks + part] = high
            a_low[place * col_blocks + part] = low


def prepare_kernel(n_col, sibs, nbk, col_blocks, scalars, dinv, *refs):
    far = n_col // 2
    normed, own, partner = refs[:2], refs[2], refs[3]
    mine, theirs = refs[4 : 3 + far], refs[3 + far : 2 + 2 * far]
    n_high, n_low, a_high, a_low, base_out = refs[2 + 2 * far :]
    col_id, wave_id, core = scalars[scalars.shape[0] - 5 + 0], scalars[scalars.shape[0] - 5 + 1], scalars[scalars.shape[0] - 5 + 2]
    half = sibs // 2
    for ref, who in zip(normed, (core, 1 - core)):
        for slot in range(nbk):
            high, low = split(ref[slot])
            n_high[slot, pl.ds(who * half, half)] = high
            n_low[slot, pl.ds(who * half, half)] = low
    here = pl.ds(pl.multiple_of(col_id * BLK, BLK), BLK)
    for step in range(far):
        places = [step * 2 + wave_id, step * 2 + 1 - wave_id]
        if step:
            put_rows(step, places, (mine[step - 1], theirs[step - 1]), col_blocks, a_high, a_low)
        else:
            put_rows(step, places, (own, partner), col_blocks, a_high, a_low, here)
    bases = []
    for s in range(sibs):
        factor = split(dinv[s])
        bases.append(packed_product(factor, factor, CONTRACT_FIRST))
    for i in range(half // 2):
        for first in (0, half):
            base_out[first // 2 + i] = jnp.concatenate([bases[first + i], bases[first + half // 2 + i]], axis=1)


def panel_kernel(n_col, sibs, nbk, col_blocks, scalars, n_high, n_low, early_high, early_low, *refs):
    far = n_col // 2
    mine, theirs = refs[: n_col - far], refs[n_col - far : 2 * (n_col - far)]
    panel_out, a_high, a_low, held, sems = refs[2 * (n_col - far) :]
    col_id, wave_id, core, block = scalars[scalars.shape[0] - 5 + 0], scalars[scalars.shape[0] - 5 + 1], scalars[scalars.shape[0] - 5 + 2], scalars[scalars.shape[0] - 5 + 4]
    group = 2 * col_blocks
    for step in range(far):
        for part in range(group):
            a_high[(col_id ^ step) * group + part] = early_high[step * group + part]
            a_low[(col_id ^ step) * group + part] = early_low[step * group + part]
    for i, step in enumerate(range(far, n_col)):
        places = [(col_id ^ step) * 2 + wave_id, (col_id ^ step) * 2 + 1 - wave_id]
        put_rows(step, places, (mine[i], theirs[i]), col_blocks, a_high, a_low)

    def sibling(s, carry):
        total = jnp.zeros((n_high.shape[2], BLK), jnp.float32)
        found = False
        width = min(4, nbk)
        for first in range(0, nbk, width):
            places = [scalars[(s) * nbk + first + k] for k in range(width)]
            left = tuple(jnp.concatenate([ref[first + k, s] for k in range(width)], axis=1) for ref in (n_high, n_low))
            right = tuple(jnp.concatenate([ref[place] for place in places], axis=1) for ref in (a_high, a_low))
            total = total + packed_product(left, right, CONTRACT_LAST)
            for place in places:
                found = jnp.logical_or(found, place == block)
        held[s] = total * jnp.where(found, -1.0, 0.0)
        pltpu.make_async_copy(held.at[s], panel_out.at[s], sems.at[s]).start()
        return carry

    if sibs * nbk <= 64:
        for s in range(sibs):
            sibling(s, 0)
    else:
        lax.fori_loop(0, sibs, sibling, 0)
    for s in range(sibs):
        pltpu.make_async_copy(held.at[s], panel_out.at[s], sems.at[s]).wait()


def per_device(lower_panel, diag_inverse, ancestor_inverse, pattern):
    sibs, width, packed = lower_panel.shape
    rows_here, cols_here = ancestor_inverse.shape
    n_row, n_col = lax.axis_size("row"), lax.axis_size("col")
    row_id, col_id, wave_id = (lax.axis_index(axis) for axis in ("row", "col", "wave"))
    core = row_id % 2
    own_rows = rows_here // n_col
    slots, col_blocks, nbk = packed // BLK, cols_here // BLK, pattern.shape[1]
    rows_blocks = rows_here // BLK
    half, quarter = sibs // 2, sibs // 4
    n_blocks = n_col * 2 * col_blocks
    f32, bf16 = jnp.float32, jnp.bfloat16
    smem = pl.BlockSpec(memory_space=pltpu.SMEM)
    vmem = pl.BlockSpec(memory_space=pltpu.VMEM)
    mib = 2**20
    size = rows_here * cols_here * 4 // mib + 1
    params = pltpu.CompilerParams(vmem_limit_bytes=min(60, 12 + 12 * size) * mib)
    ids = jnp.stack([col_id, wave_id, core, row_id, row_id * n_col + col_id]).astype(jnp.int32)

    def call(kernel, out_shape, operands, scratch, flops, out_space=vmem):
        moved = sum(x.size * 4 for x in operands)
        return pl.pallas_call(
            kernel,
            out_shape=out_shape,
            in_specs=[smem] + [vmem] * len(operands),
            out_specs=jax.tree.map(lambda _: out_space, out_shape),
            scratch_shapes=scratch,
            compiler_params=params,
            cost_estimate=pl.CostEstimate(flops=flops, bytes_accessed=(moved if flops > 10 else 1), transcendentals=0),
        )(scalars, *operands)

    def tie(point, value):
        names = [name for name in late if due(name) == point]
        if names:
            value, *tied = lax.optimization_barrier((value, *[late[name] for name in names]))
            late.update(zip(names, tied))
        return value

    def due(name):
        if name.startswith("prep"):
            return DONE.get("prep")
        if name[-1].isdigit():
            stem = name.rstrip("0123456789")
            return DONE.get(stem + str(min(int(name[len(stem) :]), 2)))
        return DONE.get(name)

    far = n_col // 2
    late = {}
    half_panel = lax.dynamic_slice_in_dim(lower_panel, core * half, half, 0)
    source = ancestor_inverse
    if GATE.get("wave"):
        source, half_panel = lax.optimization_barrier((source, half_panel))
    partner = xor_permute(source, "wave", 1)
    halves = {0: half_panel}
    halves[far] = xor_permute(halves[0], "col", far)
    chunks = [
        lax.dynamic_slice_in_dim(ancestor_inverse, (col_id ^ step) * own_rows, own_rows, 0) for step in range(1, n_col)
    ]
    if GATE.get("slices"):
        half_panel, *chunks = lax.optimization_barrier((half_panel, *chunks))
        halves[0] = half_panel
        halves[far] = xor_permute(half_panel, "col", far)
    gated = [i for i in range(n_col - 1) if GATE.get("mine" + str(min(i, 2))) == 1]
    if gated:
        halves[far], *held = lax.optimization_barrier((halves[far], *[chunks[i] for i in gated]))
        for i, chunk in zip(gated, held):
            chunks[i] = chunk
    held_back = [i for i in range(n_col - 1) if GATE.get("mine" + str(min(i, 2))) == 2]
    for i in range(n_col - 1):
        if i not in held_back:
            late["mine" + str(i)] = xor_permute(chunks[i], "col", i + 1)
            if not TIED:
                late["theirs" + str(i)] = xor_permute(late["mine" + str(i)], "wave", 1)
    late["core_own"] = xor_permute(ancestor_inverse, "row", 1)
    scalars = jnp.concatenate([pattern.reshape(-1), ids])
    if GATE.get("scalars"):
        halves[far], scalars = lax.optimization_barrier((halves[far], scalars))
    halves[far] = tie(0, halves[far])
    halves[far] = call(norm_kernel, jax.ShapeDtypeStruct(half_panel.shape, f32), [diag_inverse, halves[far]], [], 100000000000)
    halves[far] = tie(8, halves[far])
    near = halves[0]
    if GATE.get("near") == 1:
        halves[far], near = lax.optimization_barrier((halves[far], near))
    if GATE.get("near") == 2:
        near, *_ = lax.optimization_barrier((near, *chunks))
    if GATE.get("near") == 3:
        near, late["core_own"] = lax.optimization_barrier((near, late["core_own"]))
    bit = far // 2
    while bit:
        for step in list(halves):
            halves[step ^ bit] = xor_permute(halves[step] if step else near, "col", bit)
        bit //= 2
    if held_back:
        halves[n_col - 1], *held = lax.optimization_barrier((halves[n_col - 1], *[chunks[i] for i in held_back]))
        for i, chunk in zip(held_back, held):
            late["mine" + str(i)] = xor_permute(chunk, "col", i + 1)
            if not TIED:
                late["theirs" + str(i)] = xor_permute(late["mine" + str(i)], "wave", 1)
    partner, *tied = lax.optimization_barrier((partner, *[halves[step] for step in range(n_col)]))
    halves = dict(enumerate(tied))
    partner = tie(1, partner)
    core_partner = xor_permute(partner, "row", 1)
    if SPLIT:
        square = half * width
        partial, normed, *placed = call(
            functools.partial(first_kernel, n_col, slots, col_blocks, rows_blocks),
            (
                jax.ShapeDtypeStruct((square, square), f32),
                jax.ShapeDtypeStruct((nbk, half, width, BLK), f32),
                jax.ShapeDtypeStruct((2 * rows_blocks + 1, square, BLK), bf16),
                jax.ShapeDtypeStruct((2 * rows_blocks + 1, square, BLK), bf16),
                jax.ShapeDtypeStruct((2 * col_blocks + 1, square, BLK), bf16),
                jax.ShapeDtypeStruct((2 * col_blocks + 1, square, BLK), bf16),
            ),
            [diag_inverse] + [halves[step] for step in range(n_col)] + [ancestor_inverse, late["core_own"]],
            [],
            COST[0],
        )
        late["normed_other"] = xor_permute(normed, "row", 1)
        core_partner = tie(2, core_partner)
        total = call(
            functools.partial(second_kernel, half, width, col_blocks, rows_blocks),
            jax.ShapeDtypeStruct((quarter, width, 2 * width), f32),
            [partial, *placed, partner, core_partner],
            [],
            COST[2],
        )
    else:
        core_partner = tie(2, core_partner)
        total, normed = call(
            functools.partial(update_kernel, n_col, slots, col_blocks, rows_blocks),
            (
                jax.ShapeDtypeStruct((quarter, width, 2 * width), f32),
                jax.ShapeDtypeStruct((nbk, half, width, BLK), f32),
            ),
            [diag_inverse] + [halves[step] for step in range(n_col)]
            + [ancestor_inverse, partner, late["core_own"], core_partner],
            [pltpu.VMEM((2 * rows_blocks + 1, half * width, BLK), bf16)] * 2
            + [pltpu.VMEM((2 * col_blocks + 1, half * width, BLK), bf16)] * 2,
            COST[0],
        )
        late["normed_other"] = xor_permute(normed, "row", 1)
    total = tie(3, total)
    bits = [2**i for i in range(1, n_row.bit_length() - 1)]
    if RADIX:
        last = bits.pop()
    for bit in bits:
        total = total + xor_permute(total, "row", bit)
    total = tie(4, total)
    early = [diag_inverse, normed, late["normed_other"], ancestor_inverse, partner]
    early += [late[name + str(i)] for name in ("mine", "theirs") for i in range(far - 1)]
    prepared = call(
        functools.partial(prepare_kernel, n_col, sibs, nbk, col_blocks),
        (
            jax.ShapeDtypeStruct((nbk, sibs, width, BLK), bf16),
            jax.ShapeDtypeStruct((nbk, sibs, width, BLK), bf16),
            jax.ShapeDtypeStruct((n_blocks // 2, BLK, BLK), bf16),
            jax.ShapeDtypeStruct((n_blocks // 2, BLK, BLK), bf16),
            jax.ShapeDtypeStruct((half, width, 2 * width), f32),
        ),
        early,
        [],
        COST[3] if len(COST) > 3 else 10**7,
    )
    late.update({"prep" + str(i): x for i, x in enumerate(prepared)})
    bits = [2**i for i in range(n_col.bit_length() - 1)]
    if RADIX:
        first = bits.pop(0)
        both = [(r * n_col + c, (r ^ last) * n_col + (c ^ first)) for r in range(n_row) for c in range(n_col)]
        steps = [
            xor_permute(total, "row", last),
            xor_permute(total, "col", first),
            lax.ppermute(total, ("row", "col"), both),
        ]
        total = (total + steps[0]) + (steps[1] + steps[2])
        total = tie(5, total)
    for i, bit in enumerate(bits):
        if MIX:
            turn = (bit, bits[len(bits) - 1 - i])
            pairs = [(r * n_col + c, r * n_col + (c ^ turn[r % 2])) for r in range(n_row) for c in range(n_col)]
            total = total + lax.ppermute(total, ("row", "col"), pairs)
        else:
            total = total + xor_permute(total, "col", bit)
        if i == 0 and not RADIX:
            total = tie(5, total)
    total = tie(6, total)
    panel = call(
        functools.partial(panel_kernel, n_col, sibs, nbk, col_blocks),
        jax.ShapeDtypeStruct((sibs, width, BLK), f32),
        [late["prep" + str(i)] for i in range(4)]
        + [late[name + str(i)] for name in ("mine", "theirs") for i in range(far - 1, n_col - 1)],
        [
            pltpu.VMEM((n_blocks, BLK, BLK), bf16),
            pltpu.VMEM((n_blocks, BLK, BLK), bf16),
            pltpu.VMEM((sibs, width, BLK), f32),
            pltpu.SemaphoreType.DMA((sibs,)),
        ],
        COST[1],
        pl.BlockSpec(memory_space=pl.ANY),
    )
    base = late["prep4"]
    if DONE.get("panel") == 6:
        total, panel = lax.optimization_barrier((total, panel))
    other = xor_permute(total, "row", 1)
    if DONE.get("panel") == 7:
        other, panel = lax.optimization_barrier((other, panel))
    first = jnp.where(core == 0, total, other) + base[:quarter]
    second = jnp.where(core == 0, other, total) + base[quarter:]
    diag = jnp.concatenate([first[..., :width], first[..., width:], second[..., :width], second[..., width:]], axis=0)
    return panel, diag


def solution(mesh):
    return jax.shard_map(
        per_device,
        mesh=mesh,
        in_specs=(
            P("wave", None, "col"),
            P("wave", None, None),
            P("row", ("col", "wave")),
            P("wave", None),
        ),
        out_specs=(P("wave", None, ("row", "col")), P("wave", None, None)),
        check_vma=False,
    )
```

```python
import functools

import jax
import jax.numpy as jnp
from jax import lax
from jax.experimental import pallas as pl
from jax.experimental.pallas import tpu as pltpu
from jax.sharding import PartitionSpec as P

BLK = 128
CONTRACT_LAST = ((1,), (1,))
CONTRACT_FIRST = ((0,), (0,))


DONE = {'core_own': 2, 'mine0': 2, 'mine1': 5, 'mine2': 3, 'normed_other': 4, 'panel': 6, 'prep': 4, 'theirs0': 5, 'theirs1': None, 'theirs2': None}
GATE = {'mine0': 0, 'mine2': False, 'scalars': True}
SPLIT = True
RADIX = False
MIX = False
TIED = False
COST = [100000000000, 100000000000, 100000000000]


def xor_permute(value, axis, distance):
    return lax.ppermute(value, axis, [(i, i ^ distance) for i in range(lax.axis_size(axis))])


def split(value):
    high = value.astype(jnp.bfloat16)
    return high, (value - high.astype(jnp.float32)).astype(jnp.bfloat16)


def product(left, right, dims):
    dot = functools.partial(lax.dot_general, dimension_numbers=(dims, ((), ())), preferred_element_type=jnp.float32)
    return dot(left[0], right[0]) + (dot(left[0], right[1]) + dot(left[1], right[0]))


def norm_kernel(scalars, dinv, lower, out):
    half = out.shape[0]
    core = scalars[scalars.shape[0] - 3]
    for s in range(half):
        out[s] = product(split(dinv[core * half + s]), split(lower[s]), CONTRACT_FIRST)


def packed_product(left, right, dims):
    axis = 1 - dims[0][0]
    rows, columns = left[0].shape[axis], right[0].shape[axis]
    both = lax.dot_general(
        jnp.concatenate(left, axis=axis),
        jnp.concatenate(right, axis=axis),
        (dims, ((), ())),
        preferred_element_type=jnp.float32,
    )
    return both[:rows, :columns] + (both[:rows, columns:] + both[rows:, :columns])


def update_kernel(n_col, slots, col_blocks, rows_blocks, scalars, dinv, *refs):
    halves, (own, partner, core_own, core_partner) = refs[:n_col], refs[n_col : n_col + 4]
    out, normed_out, r_high, r_low, c_high, c_low = refs[n_col + 4 :]
    nbk = n_col * slots
    col_id, wave_id, core, row_id = scalars[scalars.shape[0] - 5 + 0], scalars[scalars.shape[0] - 5 + 1], scalars[scalars.shape[0] - 5 + 2], scalars[scalars.shape[0] - 5 + 3]
    half, width = halves[0].shape[0], halves[0].shape[1]
    row_first = (row_id - core) * rows_blocks
    col_first = col_id * 2 * col_blocks
    n_rows, n_cols = 2 * rows_blocks, 2 * col_blocks
    for ref in (r_high, r_low, c_high, c_low):
        ref[...] = jnp.zeros_like(ref)
    for s in range(half):
        far = n_col // 2
        lower = jnp.concatenate([halves[step][s] for step in range(far)], axis=1)
        normed = packed_product(split(dinv[core * half + s]), split(lower), CONTRACT_FIRST)
        normed = jnp.concatenate([normed] + [halves[step][s] for step in range(far, n_col)], axis=1)
        for step in range(n_col):
            for slot in range(slots):
                first = (step * slots + slot) * BLK
                here = normed[:, first : first + BLK]
                number = (col_id ^ step) * slots + slot
                normed_out[number, s] = here
                high, low = split(here)
                place = scalars[(core * half + s) * nbk + number]
                for first, count, to_high, to_low in ((row_first, n_rows, r_high, r_low), (col_first, n_cols, c_high, c_low)):
                    inside = jnp.logical_and(place >= first, place < first + count)
                    target = jnp.where(inside, place - first, count)
                    to_high[target, s * width : (s + 1) * width] = high
                    to_low[target, s * width : (s + 1) * width] = low

    def columns(ref):
        mine = [ref[wave_id * col_blocks + part] for part in range(col_blocks)]
        theirs = [ref[(1 - wave_id) * col_blocks + part] for part in range(col_blocks)]
        return jnp.concatenate(mine + theirs, axis=1)

    left = columns(c_high), columns(c_low)
    total = jnp.zeros((half * width, half * width), jnp.float32)
    group = 2
    for who, mine, theirs in ((core, own, partner), (1 - core, core_own, core_partner)):
        for first in range(0, rows_blocks, group):
            rows = slice(first * BLK, (first + group) * BLK)
            block = split(jnp.concatenate([mine[rows, :], theirs[rows, :]], axis=1))
            part = product(left, block, CONTRACT_LAST)
            place = who * rows_blocks + first
            right = tuple(jnp.concatenate([ref[place + i] for i in range(group)], axis=1) for ref in (r_high, r_low))
            total = total + product(right, split(part), CONTRACT_LAST)
    blocks = [total[s * width : (s + 1) * width, s * width : (s + 1) * width] for s in range(half)]
    for i in range(half // 2):
        out[i] = jnp.concatenate([blocks[i], blocks[i + half // 2]], axis=1)


def add_products(total, left, r_high, r_low, blocks):
    for place, rows in blocks:
        part = product(left, split(rows), CONTRACT_LAST)
        right = tuple(jnp.concatenate([ref[place], ref[place + 1]], axis=1) for ref in (r_high, r_low))
        total = total + product(right, split(part), CONTRACT_LAST)
    return total


def row_pairs(core, rows_blocks, own, other):
    for who, ref in ((core, own), (1 - core, other)):
        for first in range(0, rows_blocks, 2):
            yield who * rows_blocks + first, ref[first * BLK : (first + 2) * BLK, :]


def columns(ref, first, count):
    return jnp.concatenate([ref[first + part] for part in range(count)], axis=1)


def first_kernel(n_col, slots, col_blocks, rows_blocks, scalars, dinv, *refs):
    halves, own, core_own = refs[:n_col], refs[n_col], refs[n_col + 1]
    total_out, normed_out, r_high, r_low, c_high, c_low = refs[n_col + 2 :]
    nbk = n_col * slots
    col_id, wave_id, core, row_id = scalars[scalars.shape[0] - 5 + 0], scalars[scalars.shape[0] - 5 + 1], scalars[scalars.shape[0] - 5 + 2], scalars[scalars.shape[0] - 5 + 3]
    half, width = halves[0].shape[0], halves[0].shape[1]
    row_first = (row_id - core) * rows_blocks
    col_first = col_id * 2 * col_blocks
    n_rows, n_cols = 2 * rows_blocks, 2 * col_blocks
    for ref in (r_high, r_low, c_high, c_low):
        ref[...] = jnp.zeros_like(ref)
    for s in range(half):
        far = n_col // 2
        lower = jnp.concatenate([halves[step][s] for step in range(far)], axis=1)
        normed = packed_product(split(dinv[core * half + s]), split(lower), CONTRACT_FIRST)
        normed = jnp.concatenate([normed] + [halves[step][s] for step in range(far, n_col)], axis=1)
        for step in range(n_col):
            for slot in range(slots):
                first = (step * slots + slot) * BLK
                here = normed[:, first : first + BLK]
                number = (col_id ^ step) * slots + slot
                normed_out[number, s] = here
                high, low = split(here)
                place = scalars[(core * half + s) * nbk + number]
                for first, count, to_high, to_low in ((row_first, n_rows, r_high, r_low), (col_first, n_cols, c_high, c_low)):
                    inside = jnp.logical_and(place >= first, place < first + count)
                    target = jnp.where(inside, place - first, count)
                    to_high[target, s * width : (s + 1) * width] = high
                    to_low[target, s * width : (s + 1) * width] = low
    left = tuple(columns(ref, wave_id * col_blocks, col_blocks) for ref in (c_high, c_low))
    total = jnp.zeros((half * width, half * width), jnp.float32)
    total_out[...] = add_products(total, left, r_high, r_low, row_pairs(core, rows_blocks, own, core_own))


def second_kernel(half, width, col_blocks, rows_blocks, scalars, total, r_high, r_low, c_high, c_low, partner, core_partner, out):
    wave_id, core = scalars[scalars.shape[0] - 5 + 1], scalars[scalars.shape[0] - 5 + 2]
    left = tuple(columns(ref, (1 - wave_id) * col_blocks, col_blocks) for ref in (c_high, c_low))
    total = add_products(total[...], left, r_high, r_low, row_pairs(core, rows_blocks, partner, core_partner))
    blocks = [total[s * width : (s + 1) * width, s * width : (s + 1) * width] for s in range(half)]
    for i in range(half // 2):
        out[i] = jnp.concatenate([blocks[i], blocks[i + half // 2]], axis=1)


def put_rows(step, places, sources, col_blocks, a_high, a_low, rows=None):
    for place, source in zip(places, sources):
        for part in range(col_blocks):
            inside = slice(part * BLK, (part + 1) * BLK)
            high, low = split(source[:, inside] if rows is None else source[rows, inside])
            a_high[place * col_blocks + part] = high
            a_low[place * col_blocks + part] = low


def prepare_kernel(n_col, sibs, nbk, col_blocks, scalars, dinv, *refs):
    far = n_col // 2
    normed, own, partner = refs[:2], refs[2], refs[3]
    mine, theirs = refs[4 : 3 + far], refs[3 + far : 2 + 2 * far]
    n_high, n_low, a_high, a_low, base_out = refs[2 + 2 * far :]
    col_id, wave_id, core = scalars[scalars.shape[0] - 5 + 0], scalars[scalars.shape[0] - 5 + 1], scalars[scalars.shape[0] - 5 + 2]
    half = sibs // 2
    for ref, who in zip(normed, (core, 1 - core)):
        for slot in range(nbk):
            high, low = split(ref[slot])
            n_high[slot, pl.ds(who * half, half)] = high
            n_low[slot, pl.ds(who * half, half)] = low
    here = pl.ds(pl.multiple_of(col_id * BLK, BLK), BLK)
    for step in range(far):
        places = [step * 2 + wave_id, step * 2 + 1 - wave_id]
        if step:
            put_rows(step, places, (mine[step - 1], theirs[step - 1]), col_blocks, a_high, a_low)
        else:
            put_rows(step, places, (own, partner), col_blocks, a_high, a_low, here)
    bases = []
    for s in range(sibs):
        factor = split(dinv[s])
        bases.append(packed_product(factor, factor, CONTRACT_FIRST))
    for i in range(half // 2):
        for first in (0, half):
            base_out[first // 2 + i] = jnp.concatenate([bases[first + i], bases[first + half // 2 + i]], axis=1)


def panel_kernel(n_col, sibs, nbk, col_blocks, scalars, n_high, n_low, early_high, early_low, *refs):
    far = n_col // 2
    mine, theirs = refs[: n_col - far], refs[n_col - far : 2 * (n_col - far)]
    panel_out, a_high, a_low, held, sems = refs[2 * (n_col - far) :]
    col_id, wave_id, core, block = scalars[scalars.shape[0] - 5 + 0], scalars[scalars.shape[0] - 5 + 1], scalars[scalars.shape[0] - 5 + 2], scalars[scalars.shape[0] - 5 + 4]
    group = 2 * col_blocks
    for step in range(far):
        for part in range(group):
            a_high[(col_id ^ step) * group + part] = early_high[step * group + part]
            a_low[(col_id ^ step) * group + part] = early_low[step * group + part]
    for i, step in enumerate(range(far, n_col)):
        places = [(col_id ^ step) * 2 + wave_id, (col_id ^ step) * 2 + 1 - wave_id]
        put_rows(step, places, (mine[i], theirs[i]), col_blocks, a_high, a_low)

    def sibling(s, carry):
        total = jnp.zeros((n_high.shape[2], BLK), jnp.float32)
        found = False
        width = min(4, nbk)
        for first in range(0, nbk, width):
            places = [scalars[(s) * nbk + first + k] for k in range(width)]
            left = tuple(jnp.concatenate([ref[first + k, s] for k in range(width)], axis=1) for ref in (n_high, n_low))
            right = tuple(jnp.concatenate([ref[place] for place in places], axis=1) for ref in (a_high, a_low))
            total = total + packed_product(left, right, CONTRACT_LAST)
            for place in places:
                found = jnp.logical_or(found, place == block)
        held[s] = total * jnp.where(found, -1.0, 0.0)
        pltpu.make_async_copy(held.at[s], panel_out.at[s], sems.at[s]).start()
        return carry

    if sibs * nbk <= 64:
        for s in range(sibs):
            sibling(s, 0)
    else:
        lax.fori_loop(0, sibs, sibling, 0)
    for s in range(sibs):
        pltpu.make_async_copy(held.at[s], panel_out.at[s], sems.at[s]).wait()


def per_device(lower_panel, diag_inverse, ancestor_inverse, pattern):
    sibs, width, packed = lower_panel.shape
    rows_here, cols_here = ancestor_inverse.shape
    n_row, n_col = lax.axis_size("row"), lax.axis_size("col")
    row_id, col_id, wave_id = (lax.axis_index(axis) for axis in ("row", "col", "wave"))
    core = row_id % 2
    own_rows = rows_here // n_col
    slots, col_blocks, nbk = packed // BLK, cols_here // BLK, pattern.shape[1]
    rows_blocks = rows_here // BLK
    half, quarter = sibs // 2, sibs // 4
    n_blocks = n_col * 2 * col_blocks
    f32, bf16 = jnp.float32, jnp.bfloat16
    smem = pl.BlockSpec(memory_space=pltpu.SMEM)
    vmem = pl.BlockSpec(memory_space=pltpu.VMEM)
    mib = 2**20
    size = rows_here * cols_here * 4 // mib + 1
    params = pltpu.CompilerParams(vmem_limit_bytes=min(60, 12 + 12 * size) * mib)
    ids = jnp.stack([col_id, wave_id, core, row_id, row_id * n_col + col_id]).astype(jnp.int32)

    def call(kernel, out_shape, operands, scratch, flops, out_space=vmem):
        moved = sum(x.size * 4 for x in operands)
        return pl.pallas_call(
            kernel,
            out_shape=out_shape,
            in_specs=[smem] + [vmem] * len(operands),
            out_specs=jax.tree.map(lambda _: out_space, out_shape),
            scratch_shapes=scratch,
            compiler_params=params,
            cost_estimate=pl.CostEstimate(flops=flops, bytes_accessed=(moved if flops > 10 else 1), transcendentals=0),
        )(scalars, *operands)

    def tie(point, value):
        names = [name for name in late if due(name) == point]
        if names:
            value, *tied = lax.optimization_barrier((value, *[late[name] for name in names]))
            late.update(zip(names, tied))
        return value

    def due(name):
        if name.startswith("prep"):
            return DONE.get("prep")
        if name[-1].isdigit():
            stem = name.rstrip("0123456789")
            return DONE.get(stem + str(min(int(name[len(stem) :]), 2)))
        return DONE.get(name)

    far = n_col // 2
    late = {}
    half_panel = lax.dynamic_slice_in_dim(lower_panel, core * half, half, 0)
    source = ancestor_inverse
    if GATE.get("wave"):
        source, half_panel = lax.optimization_barrier((source, half_panel))
    partner = xor_permute(source, "wave", 1)
    halves = {0: half_panel}
    halves[far] = xor_permute(halves[0], "col", far)
    chunks = [
        lax.dynamic_slice_in_dim(ancestor_inverse, (col_id ^ step) * own_rows, own_rows, 0) for step in range(1, n_col)
    ]
    if GATE.get("slices"):
        half_panel, *chunks = lax.optimization_barrier((half_panel, *chunks))
        halves[0] = half_panel
        halves[far] = xor_permute(half_panel, "col", far)
    gated = [i for i in range(n_col - 1) if GATE.get("mine" + str(min(i, 2))) == 1]
    if gated:
        halves[far], *held = lax.optimization_barrier((halves[far], *[chunks[i] for i in gated]))
        for i, chunk in zip(gated, held):
            chunks[i] = chunk
    held_back = [i for i in range(n_col - 1) if GATE.get("mine" + str(min(i, 2))) == 2]
    for i in range(n_col - 1):
        if i not in held_back:
            late["mine" + str(i)] = xor_permute(chunks[i], "col", i + 1)
            if not TIED:
                late["theirs" + str(i)] = xor_permute(late["mine" + str(i)], "wave", 1)
    late["core_own"] = xor_permute(ancestor_inverse, "row", 1)
    scalars = jnp.concatenate([pattern.reshape(-1), ids])
    if GATE.get("scalars"):
        halves[far], scalars = lax.optimization_barrier((halves[far], scalars))
    halves[far] = tie(0, halves[far])
    halves[far] = call(norm_kernel, jax.ShapeDtypeStruct(half_panel.shape, f32), [diag_inverse, halves[far]], [], 100000000000)
    halves[far] = tie(8, halves[far])
    near = halves[0]
    if GATE.get("near") == 1:
        halves[far], near = lax.optimization_barrier((halves[far], near))
    if GATE.get("near") == 2:
        near, *_ = lax.optimization_barrier((near, *chunks))
    if GATE.get("near") == 3:
        near, late["core_own"] = lax.optimization_barrier((near, late["core_own"]))
    bit = far // 2
    while bit:
        for step in list(halves):
            halves[step ^ bit] = xor_permute(halves[step] if step else near, "col", bit)
        bit //= 2
    if held_back:
        halves[n_col - 1], *held = lax.optimization_barrier((halves[n_col - 1], *[chunks[i] for i in held_back]))
        for i, chunk in zip(held_back, held):
            late["mine" + str(i)] = xor_permute(chunk, "col", i + 1)
            if not TIED:
                late["theirs" + str(i)] = xor_permute(late["mine" + str(i)], "wave", 1)
    partner, *tied = lax.optimization_barrier((partner, *[halves[step] for step in range(n_col)]))
    halves = dict(enumerate(tied))
    partner = tie(1, partner)
    core_partner = xor_permute(partner, "row", 1)
    if SPLIT:
        square = half * width
        partial, normed, *placed = call(
            functools.partial(first_kernel, n_col, slots, col_blocks, rows_blocks),
            (
                jax.ShapeDtypeStruct((square, square), f32),
                jax.ShapeDtypeStruct((nbk, half, width, BLK), f32),
                jax.ShapeDtypeStruct((2 * rows_blocks + 1, square, BLK), bf16),
                jax.ShapeDtypeStruct((2 * rows_blocks + 1, square, BLK), bf16),
                jax.ShapeDtypeStruct((2 * col_blocks + 1, square, BLK), bf16),
                jax.ShapeDtypeStruct((2 * col_blocks + 1, square, BLK), bf16),
            ),
            [diag_inverse] + [halves[step] for step in range(n_col)] + [ancestor_inverse, late["core_own"]],
            [],
            COST[0],
        )
        late["normed_other"] = xor_permute(normed, "row", 1)
        core_partner = tie(2, core_partner)
        total = call(
            functools.partial(second_kernel, half, width, col_blocks, rows_blocks),
            jax.ShapeDtypeStruct((quarter, width, 2 * width), f32),
            [partial, *placed, partner, core_partner],
            [],
            COST[2],
        )
    else:
        core_partner = tie(2, core_partner)
        total, normed = call(
            functools.partial(update_kernel, n_col, slots, col_blocks, rows_blocks),
            (
                jax.ShapeDtypeStruct((quarter, width, 2 * width), f32),
                jax.ShapeDtypeStruct((nbk, half, width, BLK), f32),
            ),
            [diag_inverse] + [halves[step] for step in range(n_col)]
            + [ancestor_inverse, partner, late["core_own"], core_partner],
            [pltpu.VMEM((2 * rows_blocks + 1, half * width, BLK), bf16)] * 2
            + [pltpu.VMEM((2 * col_blocks + 1, half * width, BLK), bf16)] * 2,
            COST[0],
        )
        late["normed_other"] = xor_permute(normed, "row", 1)
    total = tie(3, total)
    bits = [2**i for i in range(1, n_row.bit_length() - 1)]
    if RADIX:
        last = bits.pop()
    for bit in bits:
        total = total + xor_permute(total, "row", bit)
    total = tie(4, total)
    early = [diag_inverse, normed, late["normed_other"], ancestor_inverse, partner]
    early += [late[name + str(i)] for name in ("mine", "theirs") for i in range(far - 1)]
    prepared = call(
        functools.partial(prepare_kernel, n_col, sibs, nbk, col_blocks),
        (
            jax.ShapeDtypeStruct((nbk, sibs, width, BLK), bf16),
            jax.ShapeDtypeStruct((nbk, sibs, width, BLK), bf16),
            jax.ShapeDtypeStruct((n_blocks // 2, BLK, BLK), bf16),
            jax.ShapeDtypeStruct((n_blocks // 2, BLK, BLK), bf16),
            jax.ShapeDtypeStruct((half, width, 2 * width), f32),
        ),
        early,
        [],
        COST[3] if len(COST) > 3 else 10**7,
    )
    late.update({"prep" + str(i): x for i, x in enumerate(prepared)})
    bits = [2**i for i in range(n_col.bit_length() - 1)]
    if RADIX:
        first = bits.pop(0)
        both = [(r * n_col + c, (r ^ last) * n_col + (c ^ first)) for r in range(n_row) for c in range(n_col)]
        steps = [
            xor_permute(total, "row", last),
            xor_permute(total, "col", first),
            lax.ppermute(total, ("row", "col"), both),
        ]
        total = (total + steps[0]) + (steps[1] + steps[2])
        total = tie(5, total)
    for i, bit in enumerate(bits):
        if MIX:
            turn = (bit, bits[len(bits) - 1 - i])
            pairs = [(r * n_col + c, r * n_col + (c ^ turn[r % 2])) for r in range(n_row) for c in range(n_col)]
            total = total + lax.ppermute(total, ("row", "col"), pairs)
        else:
            total = total + xor_permute(total, "col", bit)
        if i == 0 and not RADIX:
            total = tie(5, total)
    total = tie(6, total)
    panel = call(
        functools.partial(panel_kernel, n_col, sibs, nbk, col_blocks),
        jax.ShapeDtypeStruct((sibs, width, BLK), f32),
        [late["prep" + str(i)] for i in range(4)]
        + [late[name + str(i)] for name in ("mine", "theirs") for i in range(far - 1, n_col - 1)],
        [
            pltpu.VMEM((n_blocks, BLK, BLK), bf16),
            pltpu.VMEM((n_blocks, BLK, BLK), bf16),
            pltpu.VMEM((sibs, width, BLK), f32),
            pltpu.SemaphoreType.DMA((sibs,)),
        ],
        COST[1],
        pl.BlockSpec(memory_space=pl.ANY),
    )
    base = late["prep4"]
    if DONE.get("panel") == 6:
        total, panel = lax.optimization_barrier((total, panel))
    other = xor_permute(total, "row", 1)
    if DONE.get("panel") == 7:
        other, panel = lax.optimization_barrier((other, panel))
    first = jnp.where(core == 0, total, other) + base[:quarter]
    second = jnp.where(core == 0, other, total) + base[quarter:]
    diag = jnp.concatenate([first[..., :width], first[..., width:], second[..., :width], second[..., width:]], axis=0)
    return panel, diag


def solution(mesh):
    return jax.shard_map(
        per_device,
        mesh=mesh,
        in_specs=(
            P("wave", None, "col"),
            P("wave", None, None),
            P("row", ("col", "wave")),
            P("wave", None),
        ),
        out_specs=(P("wave", None, ("row", "col")), P("wave", None, None)),
        check_vma=False,
    )
```

```python
import functools

import jax
import jax.numpy as jnp
from jax import lax
from jax.experimental import pallas as pl
from jax.experimental.pallas import tpu as pltpu
from jax.sharding import PartitionSpec as P

BLK = 128
CONTRACT_LAST = ((1,), (1,))
CONTRACT_FIRST = ((0,), (0,))


DONE = {'core_own': 2, 'mine0': 2, 'mine1': 5, 'mine2': 3, 'normed_other': 4, 'panel': 6, 'prep': None, 'theirs0': 5, 'theirs1': None, 'theirs2': None}
GATE = {'mine0': 0, 'mine2': False, 'scalars': True}
SPLIT = True
RADIX = False
MIX = True
TIED = False
COST = [100000000000, 100000000000, 100000000000]


def xor_permute(value, axis, distance):
    return lax.ppermute(value, axis, [(i, i ^ distance) for i in range(lax.axis_size(axis))])


def split(value):
    high = value.astype(jnp.bfloat16)
    return high, (value - high.astype(jnp.float32)).astype(jnp.bfloat16)


def product(left, right, dims):
    dot = functools.partial(lax.dot_general, dimension_numbers=(dims, ((), ())), preferred_element_type=jnp.float32)
    return dot(left[0], right[0]) + (dot(left[0], right[1]) + dot(left[1], right[0]))


def norm_kernel(scalars, dinv, lower, out):
    half = out.shape[0]
    core = scalars[scalars.shape[0] - 3]
    for s in range(half):
        out[s] = packed_product(split(dinv[core * half + s]), split(lower[s]), CONTRACT_FIRST)


def packed_product(left, right, dims):
    axis = 1 - dims[0][0]
    rows, columns = left[0].shape[axis], right[0].shape[axis]
    both = lax.dot_general(
        jnp.concatenate(left, axis=axis),
        jnp.concatenate(right, axis=axis),
        (dims, ((), ())),
        preferred_element_type=jnp.float32,
    )
    return both[:rows, :columns] + (both[:rows, columns:] + both[rows:, :columns])


def update_kernel(n_col, slots, col_blocks, rows_blocks, scalars, dinv, *refs):
    halves, (own, partner, core_own, core_partner) = refs[:n_col], refs[n_col : n_col + 4]
    out, normed_out, r_high, r_low, c_high, c_low = refs[n_col + 4 :]
    nbk = n_col * slots
    col_id, wave_id, core, row_id = scalars[scalars.shape[0] - 5 + 0], scalars[scalars.shape[0] - 5 + 1], scalars[scalars.shape[0] - 5 + 2], scalars[scalars.shape[0] - 5 + 3]
    half, width = halves[0].shape[0], halves[0].shape[1]
    row_first = (row_id - core) * rows_blocks
    col_first = col_id * 2 * col_blocks
    n_rows, n_cols = 2 * rows_blocks, 2 * col_blocks
    for ref in (r_high, r_low, c_high, c_low):
        ref[...] = jnp.zeros_like(ref)
    for s in range(half):
        far = n_col // 2
        lower = jnp.concatenate([halves[step][s] for step in range(far)], axis=1)
        normed = packed_product(split(dinv[core * half + s]), split(lower), CONTRACT_FIRST)
        normed = jnp.concatenate([normed] + [halves[step][s] for step in range(far, n_col)], axis=1)
        for step in range(n_col):
            for slot in range(slots):
                first = (step * slots + slot) * BLK
                here = normed[:, first : first + BLK]
                number = (col_id ^ step) * slots + slot
                normed_out[number, s] = here
                high, low = split(here)
                place = scalars[(core * half + s) * nbk + number]
                for first, count, to_high, to_low in ((row_first, n_rows, r_high, r_low), (col_first, n_cols, c_high, c_low)):
                    inside = jnp.logical_and(place >= first, place < first + count)
                    target = jnp.where(inside, place - first, count)
                    to_high[target, s * width : (s + 1) * width] = high
                    to_low[target, s * width : (s + 1) * width] = low

    def columns(ref):
        mine = [ref[wave_id * col_blocks + part] for part in range(col_blocks)]
        theirs = [ref[(1 - wave_id) * col_blocks + part] for part in range(col_blocks)]
        return jnp.concatenate(mine + theirs, axis=1)

    left = columns(c_high), columns(c_low)
    total = jnp.zeros((half * width, half * width), jnp.float32)
    group = 2
    for who, mine, theirs in ((core, own, partner), (1 - core, core_own, core_partner)):
        for first in range(0, rows_blocks, group):
            rows = slice(first * BLK, (first + group) * BLK)
            block = split(jnp.concatenate([mine[rows, :], theirs[rows, :]], axis=1))
            part = product(left, block, CONTRACT_LAST)
            place = who * rows_blocks + first
            right = tuple(jnp.concatenate([ref[place + i] for i in range(group)], axis=1) for ref in (r_high, r_low))
            total = total + product(right, split(part), CONTRACT_LAST)
    blocks = [total[s * width : (s + 1) * width, s * width : (s + 1) * width] for s in range(half)]
    for i in range(half // 2):
        out[i] = jnp.concatenate([blocks[i], blocks[i + half // 2]], axis=1)


def add_products(total, left, r_high, r_low, blocks):
    for place, rows in blocks:
        part = product(left, split(rows), CONTRACT_LAST)
        right = tuple(jnp.concatenate([ref[place], ref[place + 1]], axis=1) for ref in (r_high, r_low))
        total = total + product(right, split(part), CONTRACT_LAST)
    return total


def row_pairs(core, rows_blocks, own, other):
    for who, ref in ((core, own), (1 - core, other)):
        for first in range(0, rows_blocks, 2):
            yield who * rows_blocks + first, ref[first * BLK : (first + 2) * BLK, :]


def columns(ref, first, count):
    return jnp.concatenate([ref[first + part] for part in range(count)], axis=1)


def first_kernel(n_col, slots, col_blocks, rows_blocks, scalars, dinv, *refs):
    halves, own, core_own = refs[:n_col], refs[n_col], refs[n_col + 1]
    total_out, normed_out, r_high, r_low, c_high, c_low = refs[n_col + 2 :]
    nbk = n_col * slots
    col_id, wave_id, core, row_id = scalars[scalars.shape[0] - 5 + 0], scalars[scalars.shape[0] - 5 + 1], scalars[scalars.shape[0] - 5 + 2], scalars[scalars.shape[0] - 5 + 3]
    half, width = halves[0].shape[0], halves[0].shape[1]
    row_first = (row_id - core) * rows_blocks
    col_first = col_id * 2 * col_blocks
    n_rows, n_cols = 2 * rows_blocks, 2 * col_blocks
    for ref in (r_high, r_low, c_high, c_low):
        ref[...] = jnp.zeros_like(ref)
    for s in range(half):
        far = n_col // 2
        lower = jnp.concatenate([halves[step][s] for step in range(far)], axis=1)
        normed = packed_product(split(dinv[core * half + s]), split(lower), CONTRACT_FIRST)
        normed = jnp.concatenate([normed] + [halves[step][s] for step in range(far, n_col)], axis=1)
        for step in range(n_col):
            for slot in range(slots):
                first = (step * slots + slot) * BLK
                here = normed[:, first : first + BLK]
                number = (col_id ^ step) * slots + slot
                normed_out[number, s] = here
                high, low = split(here)
                place = scalars[(core * half + s) * nbk + number]
                for first, count, to_high, to_low in ((row_first, n_rows, r_high, r_low), (col_first, n_cols, c_high, c_low)):
                    inside = jnp.logical_and(place >= first, place < first + count)
                    target = jnp.where(inside, place - first, count)
                    to_high[target, s * width : (s + 1) * width] = high
                    to_low[target, s * width : (s + 1) * width] = low
    left = tuple(columns(ref, wave_id * col_blocks, col_blocks) for ref in (c_high, c_low))
    total = jnp.zeros((half * width, half * width), jnp.float32)
    total_out[...] = add_products(total, left, r_high, r_low, row_pairs(core, rows_blocks, own, core_own))


def second_kernel(half, width, col_blocks, rows_blocks, scalars, total, r_high, r_low, c_high, c_low, partner, core_partner, out):
    wave_id, core = scalars[scalars.shape[0] - 5 + 1], scalars[scalars.shape[0] - 5 + 2]
    left = tuple(columns(ref, (1 - wave_id) * col_blocks, col_blocks) for ref in (c_high, c_low))
    total = add_products(total[...], left, r_high, r_low, row_pairs(core, rows_blocks, partner, core_partner))
    blocks = [total[s * width : (s + 1) * width, s * width : (s + 1) * width] for s in range(half)]
    for i in range(half // 2):
        out[i] = jnp.concatenate([blocks[i], blocks[i + half // 2]], axis=1)


def put_rows(step, places, sources, col_blocks, a_high, a_low, rows=None):
    for place, source in zip(places, sources):
        for part in range(col_blocks):
            inside = slice(part * BLK, (part + 1) * BLK)
            high, low = split(source[:, inside] if rows is None else source[rows, inside])
            a_high[place * col_blocks + part] = high
            a_low[place * col_blocks + part] = low


def prepare_kernel(n_col, sibs, nbk, col_blocks, scalars, dinv, *refs):
    far = n_col // 2
    normed, own, partner = refs[:2], refs[2], refs[3]
    mine, theirs = refs[4 : 3 + far], refs[3 + far : 2 + 2 * far]
    n_high, n_low, a_high, a_low, base_out = refs[2 + 2 * far :]
    col_id, wave_id, core = scalars[scalars.shape[0] - 5 + 0], scalars[scalars.shape[0] - 5 + 1], scalars[scalars.shape[0] - 5 + 2]
    half = sibs // 2
    for ref, who in zip(normed, (core, 1 - core)):
        for slot in range(nbk):
            high, low = split(ref[slot])
            n_high[slot, pl.ds(who * half, half)] = high
            n_low[slot, pl.ds(who * half, half)] = low
    here = pl.ds(pl.multiple_of(col_id * BLK, BLK), BLK)
    for step in range(far):
        places = [step * 2 + wave_id, step * 2 + 1 - wave_id]
        if step:
            put_rows(step, places, (mine[step - 1], theirs[step - 1]), col_blocks, a_high, a_low)
        else:
            put_rows(step, places, (own, partner), col_blocks, a_high, a_low, here)
    bases = []
    for s in range(sibs):
        factor = split(dinv[s])
        bases.append(packed_product(factor, factor, CONTRACT_FIRST))
    for i in range(half // 2):
        for first in (0, half):
            base_out[first // 2 + i] = jnp.concatenate([bases[first + i], bases[first + half // 2 + i]], axis=1)


def panel_kernel(n_col, sibs, nbk, col_blocks, scalars, n_high, n_low, early_high, early_low, *refs):
    far = n_col // 2
    mine, theirs = refs[: n_col - far], refs[n_col - far : 2 * (n_col - far)]
    panel_out, a_high, a_low, held, sems = refs[2 * (n_col - far) :]
    col_id, wave_id, core, block = scalars[scalars.shape[0] - 5 + 0], scalars[scalars.shape[0] - 5 + 1], scalars[scalars.shape[0] - 5 + 2], scalars[scalars.shape[0] - 5 + 4]
    group = 2 * col_blocks
    for step in range(far):
        for part in range(group):
            a_high[(col_id ^ step) * group + part] = early_high[step * group + part]
            a_low[(col_id ^ step) * group + part] = early_low[step * group + part]
    for i, step in enumerate(range(far, n_col)):
        places = [(col_id ^ step) * 2 + wave_id, (col_id ^ step) * 2 + 1 - wave_id]
        put_rows(step, places, (mine[i], theirs[i]), col_blocks, a_high, a_low)

    def sibling(s, carry):
        total = jnp.zeros((n_high.shape[2], BLK), jnp.float32)
        found = False
        width = min(4, nbk)
        for first in range(0, nbk, width):
            places = [scalars[(s) * nbk + first + k] for k in range(width)]
            left = tuple(jnp.concatenate([ref[first + k, s] for k in range(width)], axis=1) for ref in (n_high, n_low))
            right = tuple(jnp.concatenate([ref[place] for place in places], axis=1) for ref in (a_high, a_low))
            total = total + packed_product(left, right, CONTRACT_LAST)
            for place in places:
                found = jnp.logical_or(found, place == block)
        held[s] = total * jnp.where(found, -1.0, 0.0)
        pltpu.make_async_copy(held.at[s], panel_out.at[s], sems.at[s]).start()
        return carry

    if sibs * nbk <= 64:
        for s in range(sibs):
            sibling(s, 0)
    else:
        lax.fori_loop(0, sibs, sibling, 0)
    for s in range(sibs):
        pltpu.make_async_copy(held.at[s], panel_out.at[s], sems.at[s]).wait()


def per_device(lower_panel, diag_inverse, ancestor_inverse, pattern):
    sibs, width, packed = lower_panel.shape
    rows_here, cols_here = ancestor_inverse.shape
    n_row, n_col = lax.axis_size("row"), lax.axis_size("col")
    row_id, col_id, wave_id = (lax.axis_index(axis) for axis in ("row", "col", "wave"))
    core = row_id % 2
    own_rows = rows_here // n_col
    slots, col_blocks, nbk = packed // BLK, cols_here // BLK, pattern.shape[1]
    rows_blocks = rows_here // BLK
    half, quarter = sibs // 2, sibs // 4
    n_blocks = n_col * 2 * col_blocks
    f32, bf16 = jnp.float32, jnp.bfloat16
    smem = pl.BlockSpec(memory_space=pltpu.SMEM)
    vmem = pl.BlockSpec(memory_space=pltpu.VMEM)
    mib = 2**20
    size = rows_here * cols_here * 4 // mib + 1
    params = pltpu.CompilerParams(vmem_limit_bytes=min(60, 12 + 12 * size) * mib)
    ids = jnp.stack([col_id, wave_id, core, row_id, row_id * n_col + col_id]).astype(jnp.int32)

    def call(kernel, out_shape, operands, scratch, flops, out_space=vmem):
        moved = sum(x.size * 4 for x in operands)
        return pl.pallas_call(
            kernel,
            out_shape=out_shape,
            in_specs=[smem] + [vmem] * len(operands),
            out_specs=jax.tree.map(lambda _: out_space, out_shape),
            scratch_shapes=scratch,
            compiler_params=params,
            cost_estimate=pl.CostEstimate(flops=flops, bytes_accessed=(moved if flops > 10 else 1), transcendentals=0),
        )(scalars, *operands)

    def tie(point, value):
        names = [name for name in late if due(name) == point]
        if names:
            value, *tied = lax.optimization_barrier((value, *[late[name] for name in names]))
            late.update(zip(names, tied))
        return value

    def due(name):
        if name.startswith("prep"):
            return DONE.get("prep")
        if name[-1].isdigit():
            stem = name.rstrip("0123456789")
            return DONE.get(stem + str(min(int(name[len(stem) :]), 2)))
        return DONE.get(name)

    far = n_col // 2
    late = {}
    half_panel = lax.dynamic_slice_in_dim(lower_panel, core * half, half, 0)
    source = ancestor_inverse
    if GATE.get("wave"):
        source, half_panel = lax.optimization_barrier((source, half_panel))
    partner = xor_permute(source, "wave", 1)
    halves = {0: half_panel}
    halves[far] = xor_permute(halves[0], "col", far)
    chunks = [
        lax.dynamic_slice_in_dim(ancestor_inverse, (col_id ^ step) * own_rows, own_rows, 0) for step in range(1, n_col)
    ]
    if GATE.get("slices"):
        half_panel, *chunks = lax.optimization_barrier((half_panel, *chunks))
        halves[0] = half_panel
        halves[far] = xor_permute(half_panel, "col", far)
    gated = [i for i in range(n_col - 1) if GATE.get("mine" + str(min(i, 2))) == 1]
    if gated:
        halves[far], *held = lax.optimization_barrier((halves[far], *[chunks[i] for i in gated]))
        for i, chunk in zip(gated, held):
            chunks[i] = chunk
    held_back = [i for i in range(n_col - 1) if GATE.get("mine" + str(min(i, 2))) == 2]
    for i in range(n_col - 1):
        if i not in held_back:
            late["mine" + str(i)] = xor_permute(chunks[i], "col", i + 1)
            if not TIED:
                late["theirs" + str(i)] = xor_permute(late["mine" + str(i)], "wave", 1)
    late["core_own"] = xor_permute(ancestor_inverse, "row", 1)
    scalars = jnp.concatenate([pattern.reshape(-1), ids])
    if GATE.get("scalars"):
        halves[far], scalars = lax.optimization_barrier((halves[far], scalars))
    halves[far] = tie(0, halves[far])
    halves[far] = call(norm_kernel, jax.ShapeDtypeStruct(half_panel.shape, f32), [diag_inverse, halves[far]], [], 100000000000)
    halves[far] = tie(8, halves[far])
    near = halves[0]
    if GATE.get("near") == 1:
        halves[far], near = lax.optimization_barrier((halves[far], near))
    if GATE.get("near") == 2:
        near, *_ = lax.optimization_barrier((near, *chunks))
    if GATE.get("near") == 3:
        near, late["core_own"] = lax.optimization_barrier((near, late["core_own"]))
    bit = far // 2
    while bit:
        for step in list(halves):
            halves[step ^ bit] = xor_permute(halves[step] if step else near, "col", bit)
        bit //= 2
    if held_back:
        halves[n_col - 1], *held = lax.optimization_barrier((halves[n_col - 1], *[chunks[i] for i in held_back]))
        for i, chunk in zip(held_back, held):
            late["mine" + str(i)] = xor_permute(chunk, "col", i + 1)
            if not TIED:
                late["theirs" + str(i)] = xor_permute(late["mine" + str(i)], "wave", 1)
    partner, *tied = lax.optimization_barrier((partner, *[halves[step] for step in range(n_col)]))
    halves = dict(enumerate(tied))
    partner = tie(1, partner)
    core_partner = xor_permute(partner, "row", 1)
    if SPLIT:
        square = half * width
        partial, normed, *placed = call(
            functools.partial(first_kernel, n_col, slots, col_blocks, rows_blocks),
            (
                jax.ShapeDtypeStruct((square, square), f32),
                jax.ShapeDtypeStruct((nbk, half, width, BLK), f32),
                jax.ShapeDtypeStruct((2 * rows_blocks + 1, square, BLK), bf16),
                jax.ShapeDtypeStruct((2 * rows_blocks + 1, square, BLK), bf16),
                jax.ShapeDtypeStruct((2 * col_blocks + 1, square, BLK), bf16),
                jax.ShapeDtypeStruct((2 * col_blocks + 1, square, BLK), bf16),
            ),
            [diag_inverse] + [halves[step] for step in range(n_col)] + [ancestor_inverse, late["core_own"]],
            [],
            COST[0],
        )
        late["normed_other"] = xor_permute(normed, "row", 1)
        core_partner = tie(2, core_partner)
        total = call(
            functools.partial(second_kernel, half, width, col_blocks, rows_blocks),
            jax.ShapeDtypeStruct((quarter, width, 2 * width), f32),
            [partial, *placed, partner, core_partner],
            [],
            COST[2],
        )
    else:
        core_partner = tie(2, core_partner)
        total, normed = call(
            functools.partial(update_kernel, n_col, slots, col_blocks, rows_blocks),
            (
                jax.ShapeDtypeStruct((quarter, width, 2 * width), f32),
                jax.ShapeDtypeStruct((nbk, half, width, BLK), f32),
            ),
            [diag_inverse] + [halves[step] for step in range(n_col)]
            + [ancestor_inverse, partner, late["core_own"], core_partner],
            [pltpu.VMEM((2 * rows_blocks + 1, half * width, BLK), bf16)] * 2
            + [pltpu.VMEM((2 * col_blocks + 1, half * width, BLK), bf16)] * 2,
            COST[0],
        )
        late["normed_other"] = xor_permute(normed, "row", 1)
    total = tie(3, total)
    bits = [2**i for i in range(1, n_row.bit_length() - 1)]
    if RADIX:
        last = bits.pop()
    for bit in bits:
        total = total + xor_permute(total, "row", bit)
    total = tie(4, total)
    early = [diag_inverse, normed, late["normed_other"], ancestor_inverse, partner]
    early += [late[name + str(i)] for name in ("mine", "theirs") for i in range(far - 1)]
    prepared = call(
        functools.partial(prepare_kernel, n_col, sibs, nbk, col_blocks),
        (
            jax.ShapeDtypeStruct((nbk, sibs, width, BLK), bf16),
            jax.ShapeDtypeStruct((nbk, sibs, width, BLK), bf16),
            jax.ShapeDtypeStruct((n_blocks // 2, BLK, BLK), bf16),
            jax.ShapeDtypeStruct((n_blocks // 2, BLK, BLK), bf16),
            jax.ShapeDtypeStruct((half, width, 2 * width), f32),
        ),
        early,
        [],
        COST[3] if len(COST) > 3 else 10**7,
    )
    late.update({"prep" + str(i): x for i, x in enumerate(prepared)})
    bits = [2**i for i in range(n_col.bit_length() - 1)]
    if RADIX:
        first = bits.pop(0)
        both = [(r * n_col + c, (r ^ last) * n_col + (c ^ first)) for r in range(n_row) for c in range(n_col)]
        steps = [
            xor_permute(total, "row", last),
            xor_permute(total, "col", first),
            lax.ppermute(total, ("row", "col"), both),
        ]
        total = (total + steps[0]) + (steps[1] + steps[2])
        total = tie(5, total)
    for i, bit in enumerate(bits):
        if MIX:
            turn = (bit, bits[len(bits) - 1 - i])
            pairs = [(r * n_col + c, r * n_col + (c ^ turn[r % 2])) for r in range(n_row) for c in range(n_col)]
            total = total + lax.ppermute(total, ("row", "col"), pairs)
        else:
            total = total + xor_permute(total, "col", bit)
        if i == 0 and not RADIX:
            total = tie(5, total)
    total = tie(6, total)
    panel = call(
        functools.partial(panel_kernel, n_col, sibs, nbk, col_blocks),
        jax.ShapeDtypeStruct((sibs, width, BLK), f32),
        [late["prep" + str(i)] for i in range(4)]
        + [late[name + str(i)] for name in ("mine", "theirs") for i in range(far - 1, n_col - 1)],
        [
            pltpu.VMEM((n_blocks, BLK, BLK), bf16),
            pltpu.VMEM((n_blocks, BLK, BLK), bf16),
            pltpu.VMEM((sibs, width, BLK), f32),
            pltpu.SemaphoreType.DMA((sibs,)),
        ],
        COST[1],
        pl.BlockSpec(memory_space=pl.ANY),
    )
    base = late["prep4"]
    if DONE.get("panel") == 6:
        total, panel = lax.optimization_barrier((total, panel))
    other = xor_permute(total, "row", 1)
    if DONE.get("panel") == 7:
        other, panel = lax.optimization_barrier((other, panel))
    first = jnp.where(core == 0, total, other) + base[:quarter]
    second = jnp.where(core == 0, other, total) + base[quarter:]
    diag = jnp.concatenate([first[..., :width], first[..., width:], second[..., :width], second[..., width:]], axis=0)
    return panel, diag


def solution(mesh):
    return jax.shard_map(
        per_device,
        mesh=mesh,
        in_specs=(
            P("wave", None, "col"),
            P("wave", None, None),
            P("row", ("col", "wave")),
            P("wave", None),
        ),
        out_specs=(P("wave", None, ("row", "col")), P("wave", None, None)),
        check_vma=False,
    )
```
